32 devices in a mesh: grp: 2 (over x), seq: 16 (over z, y, core).
Axes of the slice: x: 2, y: 2, z: 4, core: 2. Of those that a mesh axis runs over, the one named last changes fastest.
Arguments:
- tokens: bfloat16 [4096, 8192], P(('grp', 'seq')), may hold values from -6 to 6
- cotangent: bfloat16 [4096, 1024], P(('grp', 'seq')), may hold values from -6 to 6
- frozen_weight: bfloat16 [8192, 1024], P('seq'), may hold values from -0.0625 to 0.0625
- adapters: bfloat16 [32, 9216, 64], P('grp', 'seq'), may hold values from -0.5 to 0.5
- tile_job: int32 [32, 1], replicated, may hold values from 0 to 31
- job_slot: int32 [32], replicated, may hold values from 0 to 31, each once
Outputs:
- keys: bfloat16 [4096, 1024], P(('grp', 'seq'))
- token_gradient: bfloat16 [4096, 8192], P(('grp', 'seq'))
- grad_adapters: float32 [32, 9216, 64], P('grp', 'seq')
The draws below stay inside these ranges and needn't reach their ends.
All inputs are finite; a program needn't handle non-finite values.
Results may differ from the reference program's by a relative error of at most 0.0029.
Values may be sent and summed in bfloat16 or wider, within the bound.
A program may use at most 128 MiB of HBM per device.

```python
import jax
import jax.numpy as jnp
from jax import lax

D = 8192
KV = 1024
R = 64
TILE_ROWS = 128
JOBS = 32
TOKENS = 4096
TILES = 32


def draw_adapters(key, part):
    key = jax.random.fold_in(key, 7)
    shape = (JOBS, D + KV, R)
    rowpos = jnp.arange(D + KV)[None, :, None]
    spread = jnp.where(rowpos < D, D ** (-0.5), R ** (-0.5)).astype(jnp.float32)
    values = jax.random.truncated_normal(key, -4.0, 4.0, shape, jnp.float32)
    return jnp.clip(values * spread, -0.5, 0.5).astype(jnp.bfloat16)


def level_of(stream_key, dims, cuts, smallest, high):
    def one(dim, blocks):
        steps = jax.random.uniform(jax.random.fold_in(jax.random.fold_in(stream_key, 6), dim), (blocks,), jnp.float32, smallest / len(cuts), high / len(cuts))
        return jnp.repeat(jnp.exp(steps), dims[dim] // blocks).reshape((-1,) + (1,) * (len(dims) - dim - 1))

    gain = one(*cuts[0])
    for cut in cuts[1:]:
        gain = gain * one(*cut)
    return gain


def picks_of(stream_key, rows, count, top, lift):
    order = jax.random.permutation(jax.random.fold_in(stream_key, 1), count)
    boost = order
    for power in range(3):
        boost = boost * boost // count
    boost = boost * lift // count
    tickets = jax.random.randint(jax.random.fold_in(stream_key, 2), (rows, count), 0, 4096) + boost
    fixed_rows = jax.random.permutation(jax.random.fold_in(stream_key, 3), rows)[jnp.arange(count) % rows]
    tickets = jnp.where(jnp.arange(rows)[:, None] == fixed_rows[None, :], 1 << 14, tickets)
    merit = tickets * count + jnp.arange(count)
    return lax.top_k(merit.astype(jnp.int32), top)[1].astype(jnp.int32)


def bell_draw(stream_key, extent, width, limit, split=(), kind=jnp.bfloat16):
    factor_of = level_of(stream_key, extent, split, -0.22, 0.18) if split else 1.0
    entries = jax.random.normal(stream_key, extent, jnp.float32) * width * factor_of
    return jnp.minimum(jnp.maximum(entries, -limit), limit).astype(kind)


def setup_inputs(seed: int = 0) -> dict:
    seeds = jax.random.split(jax.random.key(seed), 7)
    tokens = bell_draw(seeds[0], (TOKENS, D), 1.0, 6.0, ((0, 32),))
    cotangent = bell_draw(seeds[1], (TOKENS, KV), 1.0, 6.0, ((0, 32),))
    frozen_weight = bell_draw(seeds[2], (D, KV), D ** -0.5, 0.0625, ((0, 16),))
    adapters = draw_adapters(jax.random.fold_in(seeds[6], 71), 0)
    tile_job = picks_of(seeds[4], TILES, JOBS, 1, 512)
    job_slot = jax.random.permutation(seeds[5], JOBS).astype(jnp.int32)
    return {"tokens": tokens, "cotangent": cotangent, "frozen_weight": frozen_weight, "adapters": adapters, "tile_job": tile_job, "job_slot": job_slot}


adapter_scale = 0.5


def reference(tokens, cotangent, frozen_weight, adapters, tile_job, job_slot):
    jobs = tile_job[:, 0]
    table = jnp.arange(JOBS, dtype=jnp.int32)
    slots = jnp.sum(jnp.where(jobs[:, None] == table[None, :], job_slot[None, :], 0), axis=1).astype(jnp.int32)
    token_tiles = tokens.reshape(TILES, TILE_ROWS, D)
    cot_tiles = cotangent.reshape(TILES, TILE_ROWS, KV)

    def step(grads, item):
        token_rows, output_gradients, slot = item
        adapter = lax.dynamic_index_in_dim(adapters, slot, 0, keepdims=False)
        down_weight = adapter[:D]
        up_weight = adapter[D:]
        base_weight = jnp.dot(token_rows, frozen_weight, preferred_element_type=jnp.float32)
        hidden_width = jnp.dot(token_rows, down_weight, preferred_element_type=jnp.float32).astype(jnp.bfloat16)
        adapter_weights = jnp.dot(hidden_width, up_weight.T, preferred_element_type=jnp.float32)
        keys = (base_weight + adapter_scale * adapter_weights).astype(jnp.bfloat16)
        backward_pass = jnp.dot(output_gradients, up_weight, preferred_element_type=jnp.float32).astype(jnp.bfloat16)
        input_gradient = jnp.dot(output_gradients, frozen_weight.T, preferred_element_type=jnp.float32)
        input_gradient = input_gradient + adapter_scale * jnp.dot(backward_pass, down_weight.T, preferred_element_type=jnp.float32)
        adapter_term = jnp.concatenate([adapter_scale * jnp.dot(token_rows.T, backward_pass, preferred_element_type=jnp.float32),
                                adapter_scale * jnp.dot(output_gradients.T, hidden_width, preferred_element_type=jnp.float32)], axis=0)
        current = lax.dynamic_index_in_dim(grads, slot, 0, keepdims=False)
        grads = lax.dynamic_update_index_in_dim(grads, current + adapter_term, slot, 0)
        return grads, (keys, input_gradient.astype(jnp.bfloat16))

    start = jnp.zeros((JOBS, D + KV, R), jnp.float32)
    grads, (keys, input_gradient) = lax.scan(step, start, (token_tiles, cot_tiles, slots))
    return keys.reshape(TOKENS, KV), input_gradient.reshape(TOKENS, D), grads
```

```python
import functools

import jax
import jax.numpy as jnp
from jax import lax
from jax.experimental import pallas as pl
from jax.experimental.pallas import tpu as pltpu
from jax.sharding import PartitionSpec as P

TILE_ROWS = 128
MESH = pl.DeviceIdType.MESH

adapter_scale = 0.5

PLANES = 4
SHARDS = 16


def nt_dot(a, b):
    return lax.dot_general(a, b, (((1,), (1,)), ((), ())), preferred_element_type=jnp.float32)


def dot(a, b):
    return jnp.dot(a, b, preferred_element_type=jnp.float32)


def exchange_kernel(
    slots_ref, tok_ref, cot_ref, w_ref, adp_ref,
    keys_ref, tg_ref, gbuf,
    wbuf, all_adp, picked, pieces, down_t, gsend, acc, back,
    w_send, w_recv, own_sem, xa_send, xa_recv, a_send, a_recv, g_send, g_recv, xg_send, xg_recv,
):
    grp = lax.axis_index("grp")
    me = lax.axis_index("seq")
    core = me % 2
    row = (me // 2) % 2
    plane = me // 4
    slot_count, rank, piece_cols = adp_ref.shape
    width = tok_ref.shape[1]
    shard_rows = width // SHARDS

    barrier = pltpu.get_barrier_semaphore()
    def greet(p, _):
        pl.semaphore_signal(barrier, inc=1, device_id=(grp, (me + p) % SHARDS), device_id_type=MESH)
        return 0
    own_copies = [
        pltpu.make_async_copy(w_ref.at[h], wbuf.at[me, h], w_recv.at[me * 2 + h]) for h in range(2)
    ]
    for copy in own_copies:
        copy.start()
    keep = pltpu.make_async_copy(adp_ref, all_adp.at[pl.ds(grp * slot_count, slot_count)], own_sem)
    keep.start()
    lax.fori_loop(1, SHARDS, greet, 0)
    pl.semaphore_signal(barrier, inc=1, device_id=(1 - grp, me), device_id_type=MESH)
    pl.semaphore_wait(barrier, SHARDS)

    def adapter_swap():
        return pltpu.make_async_remote_copy(
            adp_ref, all_adp.at[pl.ds(grp * slot_count, slot_count)], xa_send, xa_recv,
            device_id=(1 - grp, me), device_id_type=MESH)

    adapter_swap().start()

    def send_w(p, y, h, kind):
        s = p * 4 + y * 2 + core
        target = (
            (grp, me + 4), (grp, me - 4),
            (grp, plane * 4 + (1 - row) * 2 + core),
            (1 - grp, me),
            (grp, plane * 4 + row * 2 + 1 - core),
        )[kind]
        return pltpu.make_async_remote_copy(
            wbuf.at[s, h], wbuf.at[s, h],
            w_send.at[((p * 2 + y) * 2 + h) * 5 + kind], w_recv.at[s * 2 + h],
            device_id=target, device_id_type=MESH)

    def take_w(s, h):
        pltpu.make_async_copy(wbuf.at[s, h], wbuf.at[s, h], w_recv.at[s * 2 + h]).wait()

    def with_plane(k, do):
        d = (k + 1) // 2
        p = plane + d * (2 * (k % 2) - 1)
        pl.when((k >= 0) & (k < 2 * PLANES - 1) & (p >= 0) & (p < PLANES))(functools.partial(do, p))

    def along_planes(p, h, act):
        @pl.when((p <= plane) & (plane < PLANES - 1))
        def _():
            act(send_w(p, row, h, 0))

        @pl.when((p >= plane) & (plane > 0))
        def _():
            act(send_w(p, row, h, 1))

    def start(copy):
        copy.start()

    def finish(copy):
        copy.wait_send()

    def plane_step(p):
        for h in range(2):
            take_w(p * 4 + row * 2 + core, h)
            along_planes(p, h, start)

            @pl.when(grp == h)
            def _():
                send_w(p, row, h, 2).start()

            send_w(p, row, h, 4).start()

    def row_step(p):
        take_w(p * 4 + (1 - row) * 2 + core, grp)
        send_w(p, 1 - row, grp, 3).start()
        send_w(p, 1 - row, grp, 4).start()

    def group_step(p):
        take_w(p * 4 + (1 - row) * 2 + core, 1 - grp)
        send_w(p, 1 - row, 1 - grp, 4).start()

    def core_step(p):
        for y in range(2):
            for h in range(2):
                take_w(p * 4 + y * 2 + 1 - core, h)

    def drain_step(p):
        for h in range(2):
            along_planes(p, h, finish)

            @pl.when(grp == h)
            def _():
                send_w(p, row, h, 2).wait_send()

            send_w(p, row, h, 4).wait_send()
        send_w(p, 1 - row, grp, 3).wait_send()
        send_w(p, 1 - row, grp, 4).wait_send()
        send_w(p, 1 - row, 1 - grp, 4).wait_send()

    def compute_step(p):
        def shard(i, _):
            s = p * 4 + i
            cols = pl.ds(pl.multiple_of(s * shard_rows, shard_rows), shard_rows)
            block = wbuf[s].reshape(shard_rows, cot_ref.shape[1])
            acc[...] += dot(tok_ref[:, cols], block)
            grad = nt_dot(cot_ref[...], block) + adapter_scale * dot(back[...], down_t[:, cols])
            tg_ref[:, cols] = grad.astype(jnp.bfloat16)
            return 0

        lax.fori_loop(0, 4, shard, 0)

    def send_piece(k):
        return pltpu.make_async_remote_copy(
            picked.at[k], pieces.at[me], a_send.at[k], a_recv.at[me],
            device_id=(grp, k), device_id_type=MESH)

    def send_term(k):
        return pltpu.make_async_remote_copy(
            gsend.at[k], gbuf.at[grp * SHARDS + me], g_send.at[k], g_recv.at[me],
            device_id=(grp, k), device_id_type=MESH)

    def swap_term(k):
        return pltpu.make_async_remote_copy(
            gbuf.at[grp * SHARDS + k], gbuf.at[grp * SHARDS + k], xg_send.at[k], xg_recv.at[k],
            device_id=(1 - grp, me), device_id_type=MESH)

    def each_peer(do):
        def one(p, _):
            do((me + p) % SHARDS)
            return 0
        lax.fori_loop(1, SHARDS, one, 0)

    def pick():
        keep.wait()
        adapter_swap().wait_recv()

        def one(t, _):
            picked[t] = all_adp[slots_ref[grp * SHARDS + t]]
            return 0

        lax.fori_loop(0, SHARDS, one, 0)
        each_peer(lambda k: send_piece(k).start())
        pieces[me] = picked[me]

    def adapt():
        each_peer(lambda k: pltpu.make_async_copy(pieces.at[k], pieces.at[k], a_recv.at[k]).wait())
        pair = 2 * piece_cols
        for m in range(SHARDS // 2):
            down_t[:, m * pair:(m + 1) * pair] = jnp.concatenate([pieces[2 * m], pieces[2 * m + 1]], axis=1)
        up = down_t[:, width:]
        hidden = jnp.zeros((TILE_ROWS, rank), jnp.float32)
        hidden_t = jnp.zeros((rank, TILE_ROWS), jnp.float32)
        step = width // 4
        for q in range(4):
            t_cols = tok_ref[:, q * step:(q + 1) * step]
            d_cols = down_t[:, q * step:(q + 1) * step]
            hidden = hidden + nt_dot(t_cols, d_cols)
            hidden_t = hidden_t + nt_dot(d_cols, t_cols)
        hidden = hidden.astype(jnp.bfloat16)
        hidden_t = hidden_t.astype(jnp.bfloat16)
        back[...] = nt_dot(cot_ref[...], up).astype(jnp.bfloat16)
        back_t = nt_dot(up, cot_ref[...]).astype(jnp.bfloat16)
        acc[...] = adapter_scale * dot(hidden, up)
        for m in range(SHARDS // 2):
            first, last = m * pair, (m + 1) * pair
            if last <= width:
                term = dot(back_t, tok_ref[:, first:last])
            else:
                term = jnp.concatenate(
                    [dot(back_t, tok_ref[:, first:width]), dot(hidden_t, cot_ref[:, :last - width])], axis=1)
            term = adapter_scale * term
            gsend[2 * m] = term[:, :piece_cols].astype(jnp.bfloat16)
            gsend[2 * m + 1] = term[:, piece_cols:].astype(jnp.bfloat16)
        each_peer(lambda k: send_term(k).start())
        gbuf[grp * SHARDS + me] = gsend[me]
        swap_term(me).start()

    def hand_on():
        def one(k):
            pltpu.make_async_copy(gbuf.at[grp * SHARDS + k], gbuf.at[grp * SHARDS + k], g_recv.at[k]).wait()
            swap_term(k).start()
        each_peer(one)

    lags = (0, 1, 2, 3, 5)

    def turn(j, _):
        with_plane(j - lags[0], plane_step)
        with_plane(j - lags[1], row_step)
        with_plane(j - lags[2], group_step)
        with_plane(j - lags[3], core_step)
        pl.when(j == 2)(pick)
        pl.when(j == 4)(adapt)
        pl.when(j == 6)(hand_on)
        with_plane(j - lags[4], compute_step)
        return 0

    lax.fori_loop(0, 2 * PLANES - 1 + lags[4], turn, 0)
    keys_ref[...] = acc[...].astype(jnp.bfloat16)

    def drain(k, _):
        with_plane(k, drain_step)
        return 0

    lax.fori_loop(0, 2 * PLANES - 1, drain, 0)
    adapter_swap().wait_send()
    each_peer(lambda k: send_piece(k).wait_send())
    each_peer(lambda k: send_term(k).wait_send())

    def swapped(k, _):
        other = gbuf.at[(1 - grp) * SHARDS + k]
        swap_term(k).wait_send()
        pltpu.make_async_copy(other, other, xg_recv.at[k]).wait()
        return 0

    lax.fori_loop(0, SHARDS, swapped, 0)


def sum_kernel(local_ref, term_ref, out_ref):
    out_ref[...] = jnp.zeros_like(out_ref)
    slot_count = out_ref.shape[0]

    def one(t, _):
        slot = local_ref[t]

        @pl.when((slot >= 0) & (slot < slot_count))
        def _():
            out_ref[slot] += term_ref[t].astype(jnp.float32)

        return 0

    lax.fori_loop(0, term_ref.shape[0], one, 0)


def on_block(tokens, cotangent, frozen_weight, adapters, tile_job, job_slot):
    table = jnp.arange(job_slot.shape[0], dtype=jnp.int32)
    slots = jnp.sum(jnp.where(tile_job == table[None, :], job_slot[None, :], 0), axis=1).astype(jnp.int32)
    adapters_t = jnp.swapaxes(adapters, 1, 2)
    slot_count, rank, piece_cols = adapters_t.shape
    tiles = slots.shape[0]
    rows, width = tokens.shape
    key_columns = cotangent.shape[1]
    shard_rows = frozen_weight.shape[0]
    halves = frozen_weight.reshape(2, shard_rows // 2, key_columns)
    vmem = pl.BlockSpec(memory_space=pltpu.VMEM)
    smem = pl.BlockSpec(memory_space=pltpu.SMEM)
    bf16 = jnp.bfloat16
    dma = pltpu.SemaphoreType.DMA
    keys, token_gradient, terms = pl.pallas_call(
        exchange_kernel,
        out_shape=(
            jax.ShapeDtypeStruct((rows, key_columns), bf16),
            jax.ShapeDtypeStruct((rows, width), bf16),
            jax.ShapeDtypeStruct((tiles, rank, piece_cols), bf16),
        ),
        in_specs=[smem, vmem, vmem, pl.BlockSpec(memory_space=pl.ANY), vmem],
        out_specs=(vmem, vmem, vmem),
        scratch_shapes=[
            pltpu.VMEM((SHARDS, 2, shard_rows // 2, key_columns), bf16),
            pltpu.VMEM((tiles, rank, piece_cols), bf16),
            pltpu.VMEM((SHARDS, rank, piece_cols), bf16),
            pltpu.VMEM((SHARDS, rank, piece_cols), bf16),
            pltpu.VMEM((rank, SHARDS * piece_cols), bf16),
            pltpu.VMEM((SHARDS, rank, piece_cols), bf16),
            pltpu.VMEM((rows, key_columns), jnp.float32),
            pltpu.VMEM((rows, rank), bf16),
            dma((SHARDS * 5,)), dma((2 * SHARDS,)), dma, dma, dma,
            dma((SHARDS,)), dma((SHARDS,)), dma((SHARDS,)), dma((SHARDS,)), dma((SHARDS,)), dma((SHARDS,)),
        ],
        compiler_params=pltpu.CompilerParams(
            collective_id=0, has_side_effects=True, vmem_limit_bytes=50 * 1024 * 1024),
        name="exchange",
    )(slots, tokens, cotangent, halves, adapters_t)
    local = slots - lax.axis_index("grp") * slot_count
    grads = pl.pallas_call(
        sum_kernel,
        out_shape=jax.ShapeDtypeStruct((slot_count, rank, piece_cols), jnp.float32),
        in_specs=[smem, vmem],
        out_specs=vmem,
        compiler_params=pltpu.CompilerParams(vmem_limit_bytes=24 * 1024 * 1024),
        name="slot_sums",
    )(local, terms)
    return keys, token_gradient, jnp.swapaxes(grads, 1, 2)


def on_device(tokens, cotangent, frozen_weight, adapters, tile_job, job_slot):
    rank_width = tokens.shape[1]
    key_columns = cotangent.shape[1]
    rank = adapters.shape[2]
    slot_count = adapters.shape[0]
    row_count = adapters.shape[1]
    total_jobs = job_slot.shape[0]
    groups = lax.axis_size("grp")
    shards = lax.axis_size("seq")
    tiles_dev = tokens.shape[0] // TILE_ROWS
    group_index = lax.axis_index("grp")
    jobs = tile_job[:, 0]
    table = jnp.arange(total_jobs, dtype=jnp.int32)
    slots_all = jnp.sum(jnp.where(jobs[:, None] == table[None, :], job_slot[None, :], 0), axis=1)
    slots_all = slots_all.reshape(groups, shards, tiles_dev)
    group_slots = lax.dynamic_index_in_dim(slots_all, group_index, 0, keepdims=False)
    tile_slots = group_slots.T
    piece = lax.all_gather(frozen_weight, "seq", axis=0, tiled=True)
    forward_pass = jnp.dot(tokens, piece, preferred_element_type=jnp.float32)
    weight_update = jnp.einsum("nk,dk->nd", cotangent, piece, preferred_element_type=jnp.float32)
    owners = jnp.transpose(slots_all // slot_count, (0, 2, 1))
    local_slots = jnp.transpose(slots_all % slot_count, (0, 2, 1))
    picked = jnp.take(adapters, local_slots, axis=0)
    outgoing = jnp.where((owners == group_index)[..., None, None], picked, jnp.zeros_like(picked))
    arrived = lax.all_to_all(
        lax.all_to_all(outgoing, "grp", split_axis=0, concat_axis=0, tiled=True),
        "seq",
        split_axis=2,
        concat_axis=2,
        tiled=True,
    )
    fetched = jnp.sum(arrived.astype(jnp.float32), axis=0).astype(jnp.bfloat16)
    adapter_full = fetched.reshape(tiles_dev, shards * row_count, rank)
    down_weight = adapter_full[:, :rank_width]
    up_weight = adapter_full[:, rank_width:]
    token_tiles = tokens.reshape(tiles_dev, TILE_ROWS, rank_width)
    cot_tiles = cotangent.reshape(tiles_dev, TILE_ROWS, key_columns)
    hidden_width = jnp.einsum(
        "tnd,tdr->tnr", token_tiles, down_weight, preferred_element_type=jnp.float32
    ).astype(jnp.bfloat16)
    adapter_weights = jnp.einsum(
        "mhw,mow->mho", hidden_width, up_weight, preferred_element_type=jnp.float32
    )
    keys = (forward_pass + adapter_scale * adapter_weights.reshape(-1, key_columns)).astype(
        jnp.bfloat16
    )
    backward_pass = jnp.einsum(
        "tnk,tkr->tnr", cot_tiles, up_weight, preferred_element_type=jnp.float32
    ).astype(jnp.bfloat16)
    pass_through = jnp.einsum(
        "tnr,tdr->tnd", backward_pass, down_weight, preferred_element_type=jnp.float32
    )
    token_gradient = (weight_update + adapter_scale * pass_through.reshape(-1, rank_width)).astype(
        jnp.bfloat16
    )
    down_term = adapter_scale * jnp.einsum(
        "tnd,tnr->tdr", token_tiles, backward_pass, preferred_element_type=jnp.float32
    )
    up_term = adapter_scale * jnp.einsum(
        "tnk,tnr->tkr", cot_tiles, hidden_width, preferred_element_type=jnp.float32
    )
    terms = jnp.concatenate([down_term, up_term], axis=1).reshape(
        tiles_dev, shards, row_count, rank
    )
    incoming = lax.all_to_all(terms, "seq", split_axis=1, concat_axis=1, tiled=True)
    selector = (tile_slots.reshape(-1)[None, :] == table[:, None]).astype(jnp.float32)
    sums = jnp.dot(
        selector,
        incoming.reshape(tiles_dev * shards, row_count * rank),
        precision=lax.Precision.HIGHEST,
        preferred_element_type=jnp.float32,
    )
    owned = lax.psum_scatter(
        sums.reshape(total_jobs, row_count, rank), "grp", scatter_dimension=0, tiled=True
    )
    return (keys, token_gradient, owned)


def solution(mesh):
    placed = (
        P(("grp", "seq"), None),
        P(("grp", "seq"), None),
        P("seq", None),
        P("grp", "seq", None),
        P(),
        P(),
    )
    laid_out = mesh.shape["grp"] == 2 and mesh.shape["seq"] == SHARDS
    return jax.shard_map(
        on_block if laid_out else on_device,
        mesh=mesh,
        in_specs=placed,
        out_specs=(P(("grp", "seq"), None), P(("grp", "seq"), None), P("grp", "seq", None)),
        check_vma=False,
    )
```

```python
import functools

import jax
import jax.numpy as jnp
from jax import lax
from jax.experimental import pallas as pl
from jax.experimental.pallas import tpu as pltpu
from jax.sharding import PartitionSpec as P

TILE_ROWS = 128
MESH = pl.DeviceIdType.MESH

adapter_scale = 0.5

PLANES = 4
SHARDS = 16


def nt_dot(a, b):
    return lax.dot_general(a, b, (((1,), (1,)), ((), ())), preferred_element_type=jnp.float32)


def dot(a, b):
    return jnp.dot(a, b, preferred_element_type=jnp.float32)


def exchange_kernel(
    local_ref, owned_ref, tok_hbm, cot_hbm, w_ref, adp_hbm,
    keys_ref, tg_ref, gbuf,
    tok_ref, cot_ref, adp_ref,
    wbuf, lent, borrowed, picked, pieces, down_t, gsend, acc, back,
    w_send, w_recv, own_sem, xa_send, xa_recv, a_send, a_recv, g_send, g_recv, xg_send, xg_recv,
):
    grp = lax.axis_index("grp")
    me = lax.axis_index("seq")
    core = me % 2
    row = (me // 2) % 2
    plane = me // 4
    rank, piece_cols = adp_ref.shape[1:]
    width = tok_ref.shape[1]
    shard_rows = width // SHARDS

    barrier = pltpu.get_barrier_semaphore()
    def greet(p, _):
        pl.semaphore_signal(barrier, inc=1, device_id=(grp, (me + p) % SHARDS), device_id_type=MESH)
        return 0
    own_copies = [
        pltpu.make_async_copy(w_ref.at[h], wbuf.at[me, h], w_recv.at[me * 2 + h]) for h in range(2)
    ]
    adp_copy = pltpu.make_async_copy(adp_hbm, adp_ref, own_sem.at[0])
    tok_copy = pltpu.make_async_copy(tok_hbm, tok_ref, own_sem.at[1])
    cot_copy = pltpu.make_async_copy(cot_hbm, cot_ref, own_sem.at[2])
    for copy in (adp_copy, *own_copies, tok_copy, cot_copy):
        copy.start()
    lax.fori_loop(1, SHARDS, greet, 0)
    pl.semaphore_signal(barrier, inc=1, device_id=(1 - grp, me), device_id_type=MESH)
    adp_copy.wait()

    def each_peer(do, away=1):
        def one(p, _):
            do((me + away * p) % SHARDS)
            return 0
        lax.fori_loop(1, SHARDS, one, 0)

    def lend(t):
        return pltpu.make_async_remote_copy(
            lent.at[t], borrowed.at[t], xa_send.at[t], xa_recv.at[t],
            device_id=(1 - grp, me), device_id_type=MESH)

    def pick_lent(t, _):
        lent[t] = adp_ref[local_ref[(1 - grp) * SHARDS + t]]
        return 0

    lax.fori_loop(0, SHARDS, pick_lent, 0)
    pl.semaphore_wait(barrier, SHARDS)
    each_peer(lambda t: lend(t).start())
    lend(me).start()

    def send_w(p, y, h, kind):
        s = p * 4 + y * 2 + core
        target = (
            (grp, me + 4), (grp, me - 4),
            (grp, plane * 4 + (1 - row) * 2 + core),
            (1 - grp, me),
            (grp, plane * 4 + row * 2 + 1 - core),
        )[kind]
        return pltpu.make_async_remote_copy(
            wbuf.at[s, h], wbuf.at[s, h],
            w_send.at[((p * 2 + y) * 2 + h) * 5 + kind], w_recv.at[s * 2 + h],
            device_id=target, device_id_type=MESH)

    def take_w(s, h):
        pltpu.make_async_copy(wbuf.at[s, h], wbuf.at[s, h], w_recv.at[s * 2 + h]).wait()

    def with_planes(d, do):
        for sign in (-1, 1):
            p = plane + sign * d
            ok = (d >= 0) & (p >= 0) & (p < PLANES)
            if sign > 0:
                ok = ok & (d > 0)
            pl.when(ok)(functools.partial(do, p))

    def along_planes(p, h, act):
        @pl.when((p <= plane) & (plane < PLANES - 1))
        def _():
            act(send_w(p, row, h, 0))

        @pl.when((p >= plane) & (plane > 0))
        def _():
            act(send_w(p, row, h, 1))

    def start(copy):
        copy.start()

    def finish(copy):
        copy.wait_send()

    def plane_step(p):
        for h in range(2):
            take_w(p * 4 + row * 2 + core, h)
            along_planes(p, h, start)

            @pl.when(grp == h)
            def _():
                send_w(p, row, h, 2).start()

            send_w(p, row, h, 4).start()

    def row_step(p):
        take_w(p * 4 + (1 - row) * 2 + core, grp)
        send_w(p, 1 - row, grp, 3).start()
        send_w(p, 1 - row, grp, 4).start()

    def group_step(p):
        take_w(p * 4 + (1 - row) * 2 + core, 1 - grp)
        send_w(p, 1 - row, 1 - grp, 4).start()

    def core_step(p):
        for y in range(2):
            for h in range(2):
                take_w(p * 4 + y * 2 + 1 - core, h)

    def drain_step(p):
        for h in range(2):
            along_planes(p, h, finish)

            @pl.when(grp == h)
            def _():
                send_w(p, row, h, 2).wait_send()

            send_w(p, row, h, 4).wait_send()
        send_w(p, 1 - row, grp, 3).wait_send()
        send_w(p, 1 - row, grp, 4).wait_send()
        send_w(p, 1 - row, 1 - grp, 4).wait_send()

    def compute_step(p):
        def shard(i, _):
            s = p * 4 + i
            cols = pl.ds(pl.multiple_of(s * shard_rows, shard_rows), shard_rows)
            block = wbuf[s].reshape(shard_rows, cot_ref.shape[1])
            acc[...] += dot(tok_ref[:, cols], block)
            grad = nt_dot(cot_ref[...], block) + adapter_scale * dot(back[...], down_t[:, cols])
            tg_ref[:, cols] = grad.astype(jnp.bfloat16)
            return 0

        lax.fori_loop(0, 4, shard, 0)

    def send_piece(k):
        return pltpu.make_async_remote_copy(
            picked.at[k], pieces.at[me], a_send.at[k], a_recv.at[me],
            device_id=(grp, k), device_id_type=MESH)

    def send_term(k):
        return pltpu.make_async_remote_copy(
            gsend.at[k], gbuf.at[grp * SHARDS + me], g_send.at[k], g_recv.at[me],
            device_id=(grp, k), device_id_type=MESH)

    def swap_term(k):
        return pltpu.make_async_remote_copy(
            gbuf.at[grp * SHARDS + k], gbuf.at[grp * SHARDS + k], xg_send.at[k], xg_recv.at[k],
            device_id=(1 - grp, me), device_id_type=MESH)

    def pick():
        def choose(t):
            lend(t).wait_recv()
            tile = grp * SHARDS + t
            picked[t] = jnp.where(owned_ref[tile] == 1, adp_ref[local_ref[tile]], borrowed[t])

        def one(t):
            choose(t)
            send_piece(t).start()

        each_peer(one)
        choose(me)
        pieces[me] = picked[me]

    def adapt():
        tok_copy.wait()
        cot_copy.wait()
        each_peer(lambda k: pltpu.make_async_copy(pieces.at[k], pieces.at[k], a_recv.at[k]).wait(), -1)
        pair = 2 * piece_cols
        for m in range(SHARDS // 2):
            down_t[:, m * pair:(m + 1) * pair] = jnp.concatenate([pieces[2 * m], pieces[2 * m + 1]], axis=1)
        up = down_t[:, width:]
        hidden = jnp.zeros((TILE_ROWS, rank), jnp.float32)
        hidden_t = jnp.zeros((rank, TILE_ROWS), jnp.float32)
        step = width // 4
        for q in range(4):
            t_cols = tok_ref[:, q * step:(q + 1) * step]
            d_cols = down_t[:, q * step:(q + 1) * step]
            hidden = hidden + nt_dot(t_cols, d_cols)
            hidden_t = hidden_t + nt_dot(d_cols, t_cols)
        hidden = hidden.astype(jnp.bfloat16)
        hidden_t = hidden_t.astype(jnp.bfloat16)
        back[...] = nt_dot(cot_ref[...], up).astype(jnp.bfloat16)
        back_t = nt_dot(up, cot_ref[...]).astype(jnp.bfloat16)
        acc[...] = adapter_scale * dot(hidden, up)
        for m in range(SHARDS // 2):
            first, last = m * pair, (m + 1) * pair
            if last <= width:
                term = dot(back_t, tok_ref[:, first:last])
            else:
                term = jnp.concatenate(
                    [dot(back_t, tok_ref[:, first:width]), dot(hidden_t, cot_ref[:, :last - width])], axis=1)
            term = adapter_scale * term
            gsend[2 * m] = term[:, :piece_cols].astype(jnp.bfloat16)
            gsend[2 * m + 1] = term[:, piece_cols:].astype(jnp.bfloat16)
        each_peer(lambda k: send_term(k).start())
        gbuf[grp * SHARDS + me] = gsend[me]
        swap_term(me).start()

    def hand_on():
        def one(k):
            pltpu.make_async_copy(gbuf.at[grp * SHARDS + k], gbuf.at[grp * SHARDS + k], g_recv.at[k]).wait()
            swap_term(k).start()
        each_peer(one, -1)

    def turn(j, _):
        with_planes(j, plane_step)
        pl.when(j == 0)(pick)
        with_planes(j - 1, group_step)
        with_planes(j, row_step)
        with_planes(j - 1, core_step)
        pl.when(j == 1)(adapt)
        with_planes(j - 2, compute_step)
        return 0

    lax.fori_loop(0, PLANES, turn, 0)

    def tail(d, _):
        pl.when(d == PLANES - 1)(lambda: with_planes(d, group_step))
        pl.when(d == PLANES - 1)(lambda: with_planes(d, core_step))
        pl.when(d == PLANES - 1)(hand_on)
        with_planes(d, compute_step)
        return 0

    lax.fori_loop(PLANES - 2, PLANES, tail, 0)
    keys_ref[...] = acc[...].astype(jnp.bfloat16)

    def drain(d, _):
        with_planes(d, drain_step)
        return 0

    lax.fori_loop(0, PLANES, drain, 0)
    each_peer(lambda k: send_piece(k).wait_send())
    each_peer(lambda k: send_term(k).wait_send())

    def swapped(k, _):
        other = gbuf.at[(1 - grp) * SHARDS + k]
        lend(k).wait_send()
        swap_term(k).wait_send()
        pltpu.make_async_copy(other, other, xg_recv.at[k]).wait()
        return 0

    lax.fori_loop(0, SHARDS, swapped, 0)


def sum_kernel(local_ref, term_ref, out_ref):
    out_ref[...] = jnp.zeros_like(out_ref)
    slot_count = out_ref.shape[0]

    def one(t, _):
        slot = local_ref[t]

        @pl.when((slot >= 0) & (slot < slot_count))
        def _():
            out_ref[slot] += term_ref[t].astype(jnp.float32)

        return 0

    lax.fori_loop(0, term_ref.shape[0], one, 0)


def on_block(tokens, cotangent, frozen_weight, adapters, tile_job, job_slot):
    table = jnp.arange(job_slot.shape[0], dtype=jnp.int32)
    slots = jnp.sum(jnp.where(tile_job == table[None, :], job_slot[None, :], 0), axis=1).astype(jnp.int32)
    adapters_t = jnp.swapaxes(adapters, 1, 2)
    slot_count, rank, piece_cols = adapters_t.shape
    tiles = slots.shape[0]
    rows, width = tokens.shape
    key_columns = cotangent.shape[1]
    shard_rows = frozen_weight.shape[0]
    halves = frozen_weight.reshape(2, shard_rows // 2, key_columns)
    local = slots - lax.axis_index("grp") * slot_count
    near = jnp.clip(local, 0, slot_count - 1)
    owned = (local == near).astype(jnp.int32)
    vmem = pl.BlockSpec(memory_space=pltpu.VMEM)
    place = pl.BlockSpec(memory_space=pl.ANY)
    smem = pl.BlockSpec(memory_space=pltpu.SMEM)
    bf16 = jnp.bfloat16
    dma = pltpu.SemaphoreType.DMA
    keys, token_gradient, terms = pl.pallas_call(
        exchange_kernel,
        out_shape=(
            jax.ShapeDtypeStruct((rows, key_columns), bf16),
            jax.ShapeDtypeStruct((rows, width), bf16),
            jax.ShapeDtypeStruct((tiles, rank, piece_cols), bf16),
        ),
        in_specs=[smem, smem, place, place, place, place],
        out_specs=(vmem, vmem, vmem),
        scratch_shapes=[
            pltpu.VMEM(tokens.shape, bf16),
            pltpu.VMEM(cotangent.shape, bf16),
            pltpu.VMEM(adapters_t.shape, bf16),
            pltpu.VMEM((SHARDS, 2, shard_rows // 2, key_columns), bf16),
            pltpu.VMEM((SHARDS, rank, piece_cols), bf16),
            pltpu.VMEM((SHARDS, rank, piece_cols), bf16),
            pltpu.VMEM((SHARDS, rank, piece_cols), bf16),
            pltpu.VMEM((SHARDS, rank, piece_cols), bf16),
            pltpu.VMEM((rank, SHARDS * piece_cols), bf16),
            pltpu.VMEM((SHARDS, rank, piece_cols), bf16),
            pltpu.VMEM((rows, key_columns), jnp.float32),
            pltpu.VMEM((rows, rank), bf16),
            dma((SHARDS * 5,)), dma((2 * SHARDS,)), dma((3,)), dma((SHARDS,)), dma((SHARDS,)),
            dma((SHARDS,)), dma((SHARDS,)), dma((SHARDS,)), dma((SHARDS,)), dma((SHARDS,)), dma((SHARDS,)),
        ],
        compiler_params=pltpu.CompilerParams(
            collective_id=0, has_side_effects=True, vmem_limit_bytes=50 * 1024 * 1024),
        name="exchange",
    )(near, owned, tokens, cotangent, halves, adapters_t)
    grads = pl.pallas_call(
        sum_kernel,
        out_shape=jax.ShapeDtypeStruct((slot_count, rank, piece_cols), jnp.float32),
        in_specs=[smem, vmem],
        out_specs=vmem,
        compiler_params=pltpu.CompilerParams(vmem_limit_bytes=24 * 1024 * 1024),
        name="slot_sums",
    )(local, terms)
    return keys, token_gradient, jnp.swapaxes(grads, 1, 2)


def on_device(tokens, cotangent, frozen_weight, adapters, tile_job, job_slot):
    rank_width = tokens.shape[1]
    key_columns = cotangent.shape[1]
    rank = adapters.shape[2]
    slot_count = adapters.shape[0]
    row_count = adapters.shape[1]
    total_jobs = job_slot.shape[0]
    groups = lax.axis_size("grp")
    shards = lax.axis_size("seq")
    tiles_dev = tokens.shape[0] // TILE_ROWS
    group_index = lax.axis_index("grp")
    jobs = tile_job[:, 0]
    table = jnp.arange(total_jobs, dtype=jnp.int32)
    slots_all = jnp.sum(jnp.where(jobs[:, None] == table[None, :], job_slot[None, :], 0), axis=1)
    slots_all = slots_all.reshape(groups, shards, tiles_dev)
    group_slots = lax.dynamic_index_in_dim(slots_all, group_index, 0, keepdims=False)
    tile_slots = group_slots.T
    piece = lax.all_gather(frozen_weight, "seq", axis=0, tiled=True)
    forward_pass = jnp.dot(tokens, piece, preferred_element_type=jnp.float32)
    weight_update = jnp.einsum("nk,dk->nd", cotangent, piece, preferred_element_type=jnp.float32)
    owners = jnp.transpose(slots_all // slot_count, (0, 2, 1))
    local_slots = jnp.transpose(slots_all % slot_count, (0, 2, 1))
    picked = jnp.take(adapters, local_slots, axis=0)
    outgoing = jnp.where((owners == group_index)[..., None, None], picked, jnp.zeros_like(picked))
    arrived = lax.all_to_all(
        lax.all_to_all(outgoing, "grp", split_axis=0, concat_axis=0, tiled=True),
        "seq",
        split_axis=2,
        concat_axis=2,
        tiled=True,
    )
    fetched = jnp.sum(arrived.astype(jnp.float32), axis=0).astype(jnp.bfloat16)
    adapter_full = fetched.reshape(tiles_dev, shards * row_count, rank)
    down_weight = adapter_full[:, :rank_width]
    up_weight = adapter_full[:, rank_width:]
    token_tiles = tokens.reshape(tiles_dev, TILE_ROWS, rank_width)
    cot_tiles = cotangent.reshape(tiles_dev, TILE_ROWS, key_columns)
    hidden_width = jnp.einsum(
        "tnd,tdr->tnr", token_tiles, down_weight, preferred_element_type=jnp.float32
    ).astype(jnp.bfloat16)
    adapter_weights = jnp.einsum(
        "mhw,mow->mho", hidden_width, up_weight, preferred_element_type=jnp.float32
    )
    keys = (forward_pass + adapter_scale * adapter_weights.reshape(-1, key_columns)).astype(
        jnp.bfloat16
    )
    backward_pass = jnp.einsum(
        "tnk,tkr->tnr", cot_tiles, up_weight, preferred_element_type=jnp.float32
    ).astype(jnp.bfloat16)
    pass_through = jnp.einsum(
        "tnr,tdr->tnd", backward_pass, down_weight, preferred_element_type=jnp.float32
    )
    token_gradient = (weight_update + adapter_scale * pass_through.reshape(-1, rank_width)).astype(
        jnp.bfloat16
    )
    down_term = adapter_scale * jnp.einsum(
        "tnd,tnr->tdr", token_tiles, backward_pass, preferred_element_type=jnp.float32
    )
    up_term = adapter_scale * jnp.einsum(
        "tnk,tnr->tkr", cot_tiles, hidden_width, preferred_element_type=jnp.float32
    )
    terms = jnp.concatenate([down_term, up_term], axis=1).reshape(
        tiles_dev, shards, row_count, rank
    )
    incoming = lax.all_to_all(terms, "seq", split_axis=1, concat_axis=1, tiled=True)
    selector = (tile_slots.reshape(-1)[None, :] == table[:, None]).astype(jnp.float32)
    sums = jnp.dot(
        selector,
        incoming.reshape(tiles_dev * shards, row_count * rank),
        precision=lax.Precision.HIGHEST,
        preferred_element_type=jnp.float32,
    )
    owned = lax.psum_scatter(
        sums.reshape(total_jobs, row_count, rank), "grp", scatter_dimension=0, tiled=True
    )
    return (keys, token_gradient, owned)


def solution(mesh):
    placed = (
        P(("grp", "seq"), None),
        P(("grp", "seq"), None),
        P("seq", None),
        P("grp", "seq", None),
        P(),
        P(),
    )
    laid_out = mesh.shape["grp"] == 2 and mesh.shape["seq"] == SHARDS
    return jax.shard_map(
        on_block if laid_out else on_device,
        mesh=mesh,
        in_specs=placed,
        out_specs=(P(("grp", "seq"), None), P(("grp", "seq"), None), P("grp", "seq", None)),
        check_vma=False,
    )
```

```python
import functools

import jax
import jax.numpy as jnp
from jax import lax
from jax.experimental import pallas as pl
from jax.experimental.pallas import tpu as pltpu
from jax.sharding import PartitionSpec as P

TILE_ROWS = 128
MESH = pl.DeviceIdType.MESH

adapter_scale = 0.5

PLANES = 4
SHARDS = 16


def nt_dot(a, b):
    return lax.dot_general(a, b, (((1,), (1,)), ((), ())), preferred_element_type=jnp.float32)


def dot(a, b):
    return jnp.dot(a, b, preferred_element_type=jnp.float32)


def exchange_kernel(
    local_ref, owned_ref, tok_hbm, cot_hbm, w_ref, adp_hbm,
    keys_ref, tg_ref, gbuf,
    tok_ref, cot_ref, adp_ref,
    wbuf, lent, borrowed, picked, pieces, down_t, gsend, acc, back, cot_t,
    w_send, w_recv, own_sem, xa_send, xa_recv, a_send, a_recv, g_send, g_recv, xg_send, xg_recv,
):
    grp = lax.axis_index("grp")
    me = lax.axis_index("seq")
    core = me % 2
    row = (me // 2) % 2
    plane = me // 4
    rank, piece_cols = adp_ref.shape[1:]
    width = tok_ref.shape[1]
    shard_rows = width // SHARDS

    barrier = pltpu.get_barrier_semaphore()
    def greet(p, _):
        pl.semaphore_signal(barrier, inc=1, device_id=(grp, (me + p) % SHARDS), device_id_type=MESH)
        return 0
    own_copies = [
        pltpu.make_async_copy(w_ref.at[h], wbuf.at[me, h], w_recv.at[me * 2 + h]) for h in range(2)
    ]
    adp_copy = pltpu.make_async_copy(adp_hbm, adp_ref, own_sem.at[0])
    tok_copy = pltpu.make_async_copy(tok_hbm, tok_ref, own_sem.at[1])
    cot_copy = pltpu.make_async_copy(cot_hbm, cot_ref, own_sem.at[2])
    for copy in (adp_copy, *own_copies, tok_copy, cot_copy):
        copy.start()
    lax.fori_loop(1, SHARDS, greet, 0)
    pl.semaphore_signal(barrier, inc=1, device_id=(1 - grp, me), device_id_type=MESH)
    adp_copy.wait()

    def each_peer(do, away=1):
        def one(p, _):
            do((me + away * p) % SHARDS)
            return 0
        lax.fori_loop(1, SHARDS, one, 0)

    def lend(t):
        return pltpu.make_async_remote_copy(
            lent.at[t], borrowed.at[t], xa_send.at[t], xa_recv.at[t],
            device_id=(1 - grp, me), device_id_type=MESH)

    def pick_lent(t, _):
        lent[t] = adp_ref[local_ref[(1 - grp) * SHARDS + t]]
        return 0

    lax.fori_loop(0, SHARDS, pick_lent, 0)
    pl.semaphore_wait(barrier, SHARDS)
    each_peer(lambda t: lend(t).start())
    lend(me).start()

    def send_w(p, y, h, kind):
        s = p * 4 + y * 2 + core
        target = (
            (grp, me + 4), (grp, me - 4),
            (grp, plane * 4 + (1 - row) * 2 + core),
            (1 - grp, me),
            (grp, plane * 4 + row * 2 + 1 - core),
        )[kind]
        return pltpu.make_async_remote_copy(
            wbuf.at[s, h], wbuf.at[s, h],
            w_send.at[((p * 2 + y) * 2 + h) * 5 + kind], w_recv.at[s * 2 + h],
            device_id=target, device_id_type=MESH)

    def take_w(s, h):
        pltpu.make_async_copy(wbuf.at[s, h], wbuf.at[s, h], w_recv.at[s * 2 + h]).wait()

    def with_planes(d, do):
        for sign in (-1, 1):
            p = plane + sign * d
            ok = (d >= 0) & (p >= 0) & (p < PLANES)
            if sign > 0:
                ok = ok & (d > 0)
            pl.when(ok)(functools.partial(do, p))

    def along_planes(p, h, act):
        @pl.when((p <= plane) & (plane < PLANES - 1))
        def _():
            act(send_w(p, row, h, 0))

        @pl.when((p >= plane) & (plane > 0))
        def _():
            act(send_w(p, row, h, 1))

    def start(copy):
        copy.start()

    def finish(copy):
        copy.wait_send()

    def plane_step(p):
        for h in range(2):
            take_w(p * 4 + row * 2 + core, h)
            along_planes(p, h, start)

            @pl.when(grp == h)
            def _():
                send_w(p, row, h, 2).start()

            send_w(p, row, h, 4).start()

    def row_step(p):
        take_w(p * 4 + (1 - row) * 2 + core, grp)
        send_w(p, 1 - row, grp, 3).start()
        send_w(p, 1 - row, grp, 4).start()

    def group_step(p):
        take_w(p * 4 + (1 - row) * 2 + core, 1 - grp)
        send_w(p, 1 - row, 1 - grp, 4).start()

    def core_step(p):
        for y in range(2):
            for h in range(2):
                take_w(p * 4 + y * 2 + 1 - core, h)

    def drain_step(p):
        for h in range(2):
            along_planes(p, h, finish)

            @pl.when(grp == h)
            def _():
                send_w(p, row, h, 2).wait_send()

            send_w(p, row, h, 4).wait_send()
        send_w(p, 1 - row, grp, 3).wait_send()
        send_w(p, 1 - row, grp, 4).wait_send()
        send_w(p, 1 - row, 1 - grp, 4).wait_send()

    def compute_step(p):
        def shard(i, _):
            s = p * 4 + i
            cols = pl.ds(pl.multiple_of(s * shard_rows, shard_rows), shard_rows)
            block = wbuf[s].reshape(shard_rows, cot_ref.shape[1])
            acc[...] += dot(tok_ref[:, cols], block)
            grad = dot(block, cot_t[...]).T + adapter_scale * dot(back[...], down_t[:, cols])
            tg_ref[:, cols] = grad.astype(jnp.bfloat16)
            return 0

        lax.fori_loop(0, 4, shard, 0)

    def send_piece(k):
        return pltpu.make_async_remote_copy(
            picked.at[k], pieces.at[me], a_send.at[k], a_recv.at[me],
            device_id=(grp, k), device_id_type=MESH)

    def send_term(k):
        return pltpu.make_async_remote_copy(
            gsend.at[k], gbuf.at[grp * SHARDS + me], g_send.at[k], g_recv.at[me],
            device_id=(grp, k), device_id_type=MESH)

    def swap_term(k):
        return pltpu.make_async_remote_copy(
            gbuf.at[grp * SHARDS + k], gbuf.at[grp * SHARDS + k], xg_send.at[k], xg_recv.at[k],
            device_id=(1 - grp, me), device_id_type=MESH)

    def pick():
        def choose(t):
            lend(t).wait_recv()
            tile = grp * SHARDS + t
            picked[t] = jnp.where(owned_ref[tile] == 1, adp_ref[local_ref[tile]], borrowed[t])

        def one(t):
            choose(t)
            send_piece(t).start()

        each_peer(one)
        choose(me)
        pieces[me] = picked[me]

    def adapt():
        tok_copy.wait()
        cot_copy.wait()
        each_peer(lambda k: pltpu.make_async_copy(pieces.at[k], pieces.at[k], a_recv.at[k]).wait(), -1)
        pair = 2 * piece_cols
        for m in range(SHARDS // 2):
            down_t[:, m * pair:(m + 1) * pair] = jnp.concatenate([pieces[2 * m], pieces[2 * m + 1]], axis=1)
        up = down_t[:, width:]
        hidden = jnp.zeros((TILE_ROWS, rank), jnp.float32)
        step = width // 4
        for q in range(4):
            t_cols = tok_ref[:, q * step:(q + 1) * step]
            d_cols = down_t[:, q * step:(q + 1) * step]
            hidden = hidden + nt_dot(t_cols, d_cols)
        hidden_t = hidden.T.astype(jnp.bfloat16)
        hidden = hidden.astype(jnp.bfloat16)
        back_wide = nt_dot(cot_ref[...], up)
        back[...] = back_wide.astype(jnp.bfloat16)
        back_t = back_wide.T.astype(jnp.bfloat16)
        cot_t[...] = cot_ref[...].T
        acc[...] = adapter_scale * dot(hidden, up)
        for m in range(SHARDS // 2):
            first, last = m * pair, (m + 1) * pair
            if last <= width:
                term = dot(back_t, tok_ref[:, first:last])
            else:
                term = jnp.concatenate(
                    [dot(back_t, tok_ref[:, first:width]), dot(hidden_t, cot_ref[:, :last - width])], axis=1)
            term = adapter_scale * term
            gsend[2 * m] = term[:, :piece_cols].astype(jnp.bfloat16)
            gsend[2 * m + 1] = term[:, piece_cols:].astype(jnp.bfloat16)
        each_peer(lambda k: send_term(k).start())
        gbuf[grp * SHARDS + me] = gsend[me]
        swap_term(me).start()

    def hand_on():
        def one(k):
            pltpu.make_async_copy(gbuf.at[grp * SHARDS + k], gbuf.at[grp * SHARDS + k], g_recv.at[k]).wait()
            swap_term(k).start()
        each_peer(one, -1)

    def turn(j, _):
        with_planes(j, plane_step)
        pl.when(j == 0)(pick)
        with_planes(j - 1, group_step)
        with_planes(j, row_step)
        with_planes(j - 1, core_step)
        pl.when(j == 1)(adapt)
        with_planes(j - 2, compute_step)
        return 0

    lax.fori_loop(0, PLANES, turn, 0)

    def tail(d, _):
        pl.when(d == PLANES - 1)(lambda: with_planes(d, group_step))
        pl.when(d == PLANES - 1)(lambda: with_planes(d, core_step))
        pl.when(d == PLANES - 1)(hand_on)
        with_planes(d, compute_step)
        return 0

    lax.fori_loop(PLANES - 2, PLANES, tail, 0)
    keys_ref[...] = acc[...].astype(jnp.bfloat16)

    def drain(d, _):
        with_planes(d, drain_step)
        return 0

    lax.fori_loop(0, PLANES, drain, 0)
    each_peer(lambda k: send_piece(k).wait_send())
    each_peer(lambda k: send_term(k).wait_send())

    def swapped(k, _):
        other = gbuf.at[(1 - grp) * SHARDS + k]
        lend(k).wait_send()
        swap_term(k).wait_send()
        pltpu.make_async_copy(other, other, xg_recv.at[k]).wait()
        return 0

    lax.fori_loop(0, SHARDS, swapped, 0)


def sum_kernel(local_ref, term_ref, out_ref):
    out_ref[...] = jnp.zeros_like(out_ref)
    slot_count = out_ref.shape[0]

    def one(t, _):
        slot = local_ref[t]

        @pl.when((slot >= 0) & (slot < slot_count))
        def _():
            out_ref[slot] += term_ref[t].astype(jnp.float32)

        return 0

    lax.fori_loop(0, term_ref.shape[0], one, 0)


def on_block(tokens, cotangent, frozen_weight, adapters, tile_job, job_slot):
    table = jnp.arange(job_slot.shape[0], dtype=jnp.int32)
    slots = jnp.sum(jnp.where(tile_job == table[None, :], job_slot[None, :], 0), axis=1).astype(jnp.int32)
    adapters_t = jnp.swapaxes(adapters, 1, 2)
    slot_count, rank, piece_cols = adapters_t.shape
    tiles = slots.shape[0]
    rows, width = tokens.shape
    key_columns = cotangent.shape[1]
    shard_rows = frozen_weight.shape[0]
    halves = frozen_weight.reshape(2, shard_rows // 2, key_columns)
    local = slots - lax.axis_index("grp") * slot_count
    near = jnp.clip(local, 0, slot_count - 1)
    owned = (local == near).astype(jnp.int32)
    vmem = pl.BlockSpec(memory_space=pltpu.VMEM)
    place = pl.BlockSpec(memory_space=pl.ANY)
    smem = pl.BlockSpec(memory_space=pltpu.SMEM)
    bf16 = jnp.bfloat16
    dma = pltpu.SemaphoreType.DMA
    keys, token_gradient, terms = pl.pallas_call(
        exchange_kernel,
        out_shape=(
            jax.ShapeDtypeStruct((rows, key_columns), bf16),
            jax.ShapeDtypeStruct((rows, width), bf16),
            jax.ShapeDtypeStruct((tiles, rank, piece_cols), bf16),
        ),
        in_specs=[smem, smem, place, place, place, place],
        out_specs=(vmem, vmem, vmem),
        scratch_shapes=[
            pltpu.VMEM(tokens.shape, bf16),
            pltpu.VMEM(cotangent.shape, bf16),
            pltpu.VMEM(adapters_t.shape, bf16),
            pltpu.VMEM((SHARDS, 2, shard_rows // 2, key_columns), bf16),
            pltpu.VMEM((SHARDS, rank, piece_cols), bf16),
            pltpu.VMEM((SHARDS, rank, piece_cols), bf16),
            pltpu.VMEM((SHARDS, rank, piece_cols), bf16),
            pltpu.VMEM((SHARDS, rank, piece_cols), bf16),
            pltpu.VMEM((rank, SHARDS * piece_cols), bf16),
            pltpu.VMEM((SHARDS, rank, piece_cols), bf16),
            pltpu.VMEM((rows, key_columns), jnp.float32),
            pltpu.VMEM((rows, rank), bf16),
            pltpu.VMEM((key_columns, rows), bf16),
            dma((SHARDS * 5,)), dma((2 * SHARDS,)), dma((3,)), dma((SHARDS,)), dma((SHARDS,)),
            dma((SHARDS,)), dma((SHARDS,)), dma((SHARDS,)), dma((SHARDS,)), dma((SHARDS,)), dma((SHARDS,)),
        ],
        compiler_params=pltpu.CompilerParams(
            collective_id=0, has_side_effects=True, vmem_limit_bytes=50 * 1024 * 1024),
        name="exchange",
    )(near, owned, tokens, cotangent, halves, adapters_t)
    grads = pl.pallas_call(
        sum_kernel,
        out_shape=jax.ShapeDtypeStruct((slot_count, rank, piece_cols), jnp.float32),
        in_specs=[smem, vmem],
        out_specs=vmem,
        compiler_params=pltpu.CompilerParams(vmem_limit_bytes=24 * 1024 * 1024),
        name="slot_sums",
    )(local, terms)
    return keys, token_gradient, jnp.swapaxes(grads, 1, 2)


def on_device(tokens, cotangent, frozen_weight, adapters, tile_job, job_slot):
    rank_width = tokens.shape[1]
    key_columns = cotangent.shape[1]
    rank = adapters.shape[2]
    slot_count = adapters.shape[0]
    row_count = adapters.shape[1]
    total_jobs = job_slot.shape[0]
    groups = lax.axis_size("grp")
    shards = lax.axis_size("seq")
    tiles_dev = tokens.shape[0] // TILE_ROWS
    group_index = lax.axis_index("grp")
    jobs = tile_job[:, 0]
    table = jnp.arange(total_jobs, dtype=jnp.int32)
    slots_all = jnp.sum(jnp.where(jobs[:, None] == table[None, :], job_slot[None, :], 0), axis=1)
    slots_all = slots_all.reshape(groups, shards, tiles_dev)
    group_slots = lax.dynamic_index_in_dim(slots_all, group_index, 0, keepdims=False)
    tile_slots = group_slots.T
    piece = lax.all_gather(frozen_weight, "seq", axis=0, tiled=True)
    forward_pass = jnp.dot(tokens, piece, preferred_element_type=jnp.float32)
    weight_update = jnp.einsum("nk,dk->nd", cotangent, piece, preferred_element_type=jnp.float32)
    owners = jnp.transpose(slots_all // slot_count, (0, 2, 1))
    local_slots = jnp.transpose(slots_all % slot_count, (0, 2, 1))
    picked = jnp.take(adapters, local_slots, axis=0)
    outgoing = jnp.where((owners == group_index)[..., None, None], picked, jnp.zeros_like(picked))
    arrived = lax.all_to_all(
        lax.all_to_all(outgoing, "grp", split_axis=0, concat_axis=0, tiled=True),
        "seq",
        split_axis=2,
        concat_axis=2,
        tiled=True,
    )
    fetched = jnp.sum(arrived.astype(jnp.float32), axis=0).astype(jnp.bfloat16)
    adapter_full = fetched.reshape(tiles_dev, shards * row_count, rank)
    down_weight = adapter_full[:, :rank_width]
    up_weight = adapter_full[:, rank_width:]
    token_tiles = tokens.reshape(tiles_dev, TILE_ROWS, rank_width)
    cot_tiles = cotangent.reshape(tiles_dev, TILE_ROWS, key_columns)
    hidden_width = jnp.einsum(
        "tnd,tdr->tnr", token_tiles, down_weight, preferred_element_type=jnp.float32
    ).astype(jnp.bfloat16)
    adapter_weights = jnp.einsum(
        "mhw,mow->mho", hidden_width, up_weight, preferred_element_type=jnp.float32
    )
    keys = (forward_pass + adapter_scale * adapter_weights.reshape(-1, key_columns)).astype(
        jnp.bfloat16
    )
    backward_pass = jnp.einsum(
        "tnk,tkr->tnr", cot_tiles, up_weight, preferred_element_type=jnp.float32
    ).astype(jnp.bfloat16)
    pass_through = jnp.einsum(
        "tnr,tdr->tnd", backward_pass, down_weight, preferred_element_type=jnp.float32
    )
    token_gradient = (weight_update + adapter_scale * pass_through.reshape(-1, rank_width)).astype(
        jnp.bfloat16
    )
    down_term = adapter_scale * jnp.einsum(
        "tnd,tnr->tdr", token_tiles, backward_pass, preferred_element_type=jnp.float32
    )
    up_term = adapter_scale * jnp.einsum(
        "tnk,tnr->tkr", cot_tiles, hidden_width, preferred_element_type=jnp.float32
    )
    terms = jnp.concatenate([down_term, up_term], axis=1).reshape(
        tiles_dev, shards, row_count, rank
    )
    incoming = lax.all_to_all(terms, "seq", split_axis=1, concat_axis=1, tiled=True)
    selector = (tile_slots.reshape(-1)[None, :] == table[:, None]).astype(jnp.float32)
    sums = jnp.dot(
        selector,
        incoming.reshape(tiles_dev * shards, row_count * rank),
        precision=lax.Precision.HIGHEST,
        preferred_element_type=jnp.float32,
    )
    owned = lax.psum_scatter(
        sums.reshape(total_jobs, row_count, rank), "grp", scatter_dimension=0, tiled=True
    )
    return (keys, token_gradient, owned)


def solution(mesh):
    placed = (
        P(("grp", "seq"), None),
        P(("grp", "seq"), None),
        P("seq", None),
        P("grp", "seq", None),
        P(),
        P(),
    )
    laid_out = mesh.shape["grp"] == 2 and mesh.shape["seq"] == SHARDS
    return jax.shard_map(
        on_block if laid_out else on_device,
        mesh=mesh,
        in_specs=placed,
        out_specs=(P(("grp", "seq"), None), P(("grp", "seq"), None), P("grp", "seq", None)),
        check_vma=False,
    )
```

```python
import functools

import jax
import jax.numpy as jnp
from jax import lax
from jax.experimental import pallas as pl
from jax.experimental.pallas import tpu as pltpu
from jax.sharding import PartitionSpec as P

TILE_ROWS = 128
MESH = pl.DeviceIdType.MESH

adapter_scale = 0.5

PLANES = 4
SHARDS = 16


def nt_dot(a, b):
    return lax.dot_general(a, b, (((1,), (1,)), ((), ())), preferred_element_type=jnp.float32)


def dot(a, b):
    return jnp.dot(a, b, preferred_element_type=jnp.float32)


def exchange_kernel(
    local_ref, owned_ref, tok_hbm, cot_hbm, w_ref, adp_hbm,
    keys_ref, tg_ref, gbuf,
    tok_ref, cot_ref, adp_ref,
    wbuf, lent, borrowed, picked, pieces, down_t, gsend, acc, back, cot_t,
    w_send, w_recv, own_sem, xa_send, xa_recv, a_send, a_recv, g_send, g_recv, xg_send, xg_recv,
):
    grp = lax.axis_index("grp")
    me = lax.axis_index("seq")
    core = me % 2
    row = (me // 2) % 2
    plane = me // 4
    rank, piece_cols = adp_ref.shape[1:]
    width = tok_ref.shape[1]
    shard_rows = width // SHARDS

    barrier = pltpu.get_barrier_semaphore()
    def greet(p, _):
        pl.semaphore_signal(barrier, inc=1, device_id=(grp, (me + p) % SHARDS), device_id_type=MESH)
        return 0
    own_copies = [
        pltpu.make_async_copy(w_ref.at[h], wbuf.at[me, h], w_recv.at[me * 2 + h]) for h in range(2)
    ]
    adp_copy = pltpu.make_async_copy(adp_hbm, adp_ref, own_sem.at[0])
    tok_copy = pltpu.make_async_copy(tok_hbm, tok_ref, own_sem.at[1])
    cot_copy = pltpu.make_async_copy(cot_hbm, cot_ref, own_sem.at[2])
    for copy in (adp_copy, *own_copies, tok_copy, cot_copy):
        copy.start()
    lax.fori_loop(1, SHARDS, greet, 0)
    pl.semaphore_signal(barrier, inc=1, device_id=(1 - grp, me), device_id_type=MESH)
    adp_copy.wait()

    def each_peer(do, away=1):
        def one(p, _):
            do((me + away * p) % SHARDS)
            return 0
        lax.fori_loop(1, SHARDS, one, 0)

    def lend(t):
        return pltpu.make_async_remote_copy(
            lent.at[t], borrowed.at[t], xa_send.at[t], xa_recv.at[t],
            device_id=(1 - grp, me), device_id_type=MESH)

    def pick_lent(t, _):
        lent[t] = adp_ref[local_ref[(1 - grp) * SHARDS + t]]
        return 0

    lax.fori_loop(0, SHARDS, pick_lent, 0)
    pl.semaphore_wait(barrier, SHARDS)
    each_peer(lambda t: lend(t).start())
    lend(me).start()

    def send_w(p, y, h, kind):
        s = p * 4 + y * 2 + core
        target = (
            (grp, me + 4), (grp, me - 4),
            (grp, plane * 4 + (1 - row) * 2 + core),
            (1 - grp, me),
            (grp, plane * 4 + row * 2 + 1 - core),
        )[kind]
        return pltpu.make_async_remote_copy(
            wbuf.at[s, h], wbuf.at[s, h],
            w_send.at[((p * 2 + y) * 2 + h) * 5 + kind], w_recv.at[s * 2 + h],
            device_id=target, device_id_type=MESH)

    def take_w(s, h):
        pltpu.make_async_copy(wbuf.at[s, h], wbuf.at[s, h], w_recv.at[s * 2 + h]).wait()

    def with_planes(d, do):
        for sign in (-1, 1):
            p = plane + sign * d
            ok = (d >= 0) & (p >= 0) & (p < PLANES)
            if sign > 0:
                ok = ok & (d > 0)
            pl.when(ok)(functools.partial(do, p))

    def along_planes(p, h, act):
        @pl.when((p <= plane) & (plane < PLANES - 1))
        def _():
            act(send_w(p, row, h, 0))

        @pl.when((p >= plane) & (plane > 0))
        def _():
            act(send_w(p, row, h, 1))

    def start(copy):
        copy.start()

    def finish(copy):
        copy.wait_send()

    def from_plane(p, act):
        along_planes(p, grp, act)
        act(send_w(p, row, grp, 2))
        pl.when(p != plane)(lambda: act(send_w(p, row, grp, 3)))
        act(send_w(p, row, grp, 4))
        pl.when(p == plane)(lambda: act(send_w(p, row, 1 - grp, 4)))

    def from_group(p, act):
        @pl.when(p != plane)
        def _():
            act(send_w(p, row, 1 - grp, 2))
            act(send_w(p, row, 1 - grp, 4))

        @pl.when(p == plane)
        def _():
            act(send_w(p, 1 - row, 1 - grp, 4))

    def from_row(p, act):
        pl.when(p == plane)(lambda: act(send_w(p, 1 - row, grp, 3)))
        act(send_w(p, 1 - row, grp, 4))

    def from_corner(p, act):
        pl.when(p != plane)(lambda: act(send_w(p, 1 - row, 1 - grp, 4)))

    def plane_step(p):
        take_w(p * 4 + row * 2 + core, grp)
        pl.when(p == plane)(lambda: take_w(p * 4 + row * 2 + core, 1 - grp))
        from_plane(p, start)

    def group_step(p):
        pl.when(p != plane)(lambda: take_w(p * 4 + row * 2 + core, 1 - grp))
        pl.when(p == plane)(lambda: take_w(p * 4 + (1 - row) * 2 + core, 1 - grp))
        from_group(p, start)

    def row_step(p):
        take_w(p * 4 + (1 - row) * 2 + core, grp)
        from_row(p, start)

    def corner_step(p):
        pl.when(p != plane)(lambda: take_w(p * 4 + (1 - row) * 2 + core, 1 - grp))
        from_corner(p, start)

    def core_step(p):
        for y in range(2):
            for h in range(2):
                take_w(p * 4 + y * 2 + 1 - core, h)

    def drain_step(p):
        for leaves in (from_plane, from_group, from_row, from_corner):
            leaves(p, finish)

    def compute_step(p):
        def shard(i, _):
            s = p * 4 + i
            cols = pl.ds(pl.multiple_of(s * shard_rows, shard_rows), shard_rows)
            block = wbuf[s].reshape(shard_rows, cot_ref.shape[1])
            acc[...] += dot(tok_ref[:, cols], block)
            grad = dot(block, cot_t[...]).T + adapter_scale * dot(back[...], down_t[:, cols])
            tg_ref[:, cols] = grad.astype(jnp.bfloat16)
            return 0

        lax.fori_loop(0, 4, shard, 0)

    def send_piece(k):
        return pltpu.make_async_remote_copy(
            picked.at[k], pieces.at[me], a_send.at[k], a_recv.at[me],
            device_id=(grp, k), device_id_type=MESH)

    def send_term(k):
        return pltpu.make_async_remote_copy(
            gsend.at[k], gbuf.at[grp * SHARDS + me], g_send.at[k], g_recv.at[me],
            device_id=(grp, k), device_id_type=MESH)

    def swap_term(k):
        return pltpu.make_async_remote_copy(
            gbuf.at[grp * SHARDS + k], gbuf.at[grp * SHARDS + k], xg_send.at[k], xg_recv.at[k],
            device_id=(1 - grp, me), device_id_type=MESH)

    def pick():
        def choose(t):
            lend(t).wait_recv()
            tile = grp * SHARDS + t
            picked[t] = jnp.where(owned_ref[tile] == 1, adp_ref[local_ref[tile]], borrowed[t])

        def one(t):
            choose(t)
            send_piece(t).start()

        each_peer(one)
        choose(me)
        pieces[me] = picked[me]

    def adapt():
        tok_copy.wait()
        cot_copy.wait()
        each_peer(lambda k: pltpu.make_async_copy(pieces.at[k], pieces.at[k], a_recv.at[k]).wait(), -1)
        pair = 2 * piece_cols
        for m in range(SHARDS // 2):
            down_t[:, m * pair:(m + 1) * pair] = jnp.concatenate([pieces[2 * m], pieces[2 * m + 1]], axis=1)
        up = down_t[:, width:]
        hidden = jnp.zeros((TILE_ROWS, rank), jnp.float32)
        step = width // 4
        for q in range(4):
            t_cols = tok_ref[:, q * step:(q + 1) * step]
            d_cols = down_t[:, q * step:(q + 1) * step]
            hidden = hidden + nt_dot(t_cols, d_cols)
        hidden_t = hidden.T.astype(jnp.bfloat16)
        hidden = hidden.astype(jnp.bfloat16)
        back_wide = nt_dot(cot_ref[...], up)
        back[...] = back_wide.astype(jnp.bfloat16)
        back_t = back_wide.T.astype(jnp.bfloat16)
        cot_t[...] = cot_ref[...].T
        acc[...] = adapter_scale * dot(hidden, up)
        for m in range(SHARDS // 2):
            first, last = m * pair, (m + 1) * pair
            if last <= width:
                term = dot(back_t, tok_ref[:, first:last])
            else:
                term = jnp.concatenate(
                    [dot(back_t, tok_ref[:, first:width]), dot(hidden_t, cot_ref[:, :last - width])], axis=1)
            term = adapter_scale * term
            gsend[2 * m] = term[:, :piece_cols].astype(jnp.bfloat16)
            gsend[2 * m + 1] = term[:, piece_cols:].astype(jnp.bfloat16)
        each_peer(lambda k: send_term(k).start())
        gbuf[grp * SHARDS + me] = gsend[me]
        swap_term(me).start()

    def hand_on():
        def one(k):
            pltpu.make_async_copy(gbuf.at[grp * SHARDS + k], gbuf.at[grp * SHARDS + k], g_recv.at[k]).wait()
            swap_term(k).start()
        each_peer(one, -1)

    def turn(j, _):
        with_planes(j, plane_step)
        pl.when(j == 0)(pick)
        with_planes(j - 1, row_step)
        with_planes(j - 1, group_step)
        pl.when(j == 1)(adapt)
        with_planes(j - 2, corner_step)
        with_planes(j - 2, core_step)
        with_planes(j - 2, compute_step)
        pl.when(j == PLANES)(hand_on)
        return 0

    lax.fori_loop(0, PLANES + 2, turn, 0)
    keys_ref[...] = acc[...].astype(jnp.bfloat16)

    def drain(d, _):
        with_planes(d, drain_step)
        return 0

    lax.fori_loop(0, PLANES, drain, 0)
    each_peer(lambda k: send_piece(k).wait_send())
    each_peer(lambda k: send_term(k).wait_send())

    def swapped(k, _):
        other = gbuf.at[(1 - grp) * SHARDS + k]
        lend(k).wait_send()
        swap_term(k).wait_send()
        pltpu.make_async_copy(other, other, xg_recv.at[k]).wait()
        return 0

    lax.fori_loop(0, SHARDS, swapped, 0)


def sum_kernel(local_ref, term_ref, out_ref):
    out_ref[...] = jnp.zeros_like(out_ref)
    slot_count = out_ref.shape[0]

    def one(t, _):
        slot = local_ref[t]

        @pl.when((slot >= 0) & (slot < slot_count))
        def _():
            out_ref[slot] += term_ref[t].astype(jnp.float32)

        return 0

    lax.fori_loop(0, term_ref.shape[0], one, 0)


def on_block(tokens, cotangent, frozen_weight, adapters, tile_job, job_slot):
    table = jnp.arange(job_slot.shape[0], dtype=jnp.int32)
    slots = jnp.sum(jnp.where(tile_job == table[None, :], job_slot[None, :], 0), axis=1).astype(jnp.int32)
    adapters_t = jnp.swapaxes(adapters, 1, 2)
    slot_count, rank, piece_cols = adapters_t.shape
    tiles = slots.shape[0]
    rows, width = tokens.shape
    key_columns = cotangent.shape[1]
    shard_rows = frozen_weight.shape[0]
    halves = frozen_weight.reshape(2, shard_rows // 2, key_columns)
    local = slots - lax.axis_index("grp") * slot_count
    near = jnp.clip(local, 0, slot_count - 1)
    owned = (local == near).astype(jnp.int32)
    vmem = pl.BlockSpec(memory_space=pltpu.VMEM)
    place = pl.BlockSpec(memory_space=pl.ANY)
    smem = pl.BlockSpec(memory_space=pltpu.SMEM)
    bf16 = jnp.bfloat16
    dma = pltpu.SemaphoreType.DMA
    keys, token_gradient, terms = pl.pallas_call(
        exchange_kernel,
        out_shape=(
            jax.ShapeDtypeStruct((rows, key_columns), bf16),
            jax.ShapeDtypeStruct((rows, width), bf16),
            jax.ShapeDtypeStruct((tiles, rank, piece_cols), bf16),
        ),
        in_specs=[smem, smem, place, place, place, place],
        out_specs=(vmem, vmem, vmem),
        scratch_shapes=[
            pltpu.VMEM(tokens.shape, bf16),
            pltpu.VMEM(cotangent.shape, bf16),
            pltpu.VMEM(adapters_t.shape, bf16),
            pltpu.VMEM((SHARDS, 2, shard_rows // 2, key_columns), bf16),
            pltpu.VMEM((SHARDS, rank, piece_cols), bf16),
            pltpu.VMEM((SHARDS, rank, piece_cols), bf16),
            pltpu.VMEM((SHARDS, rank, piece_cols), bf16),
            pltpu.VMEM((SHARDS, rank, piece_cols), bf16),
            pltpu.VMEM((rank, SHARDS * piece_cols), bf16),
            pltpu.VMEM((SHARDS, rank, piece_cols), bf16),
            pltpu.VMEM((rows, key_columns), jnp.float32),
            pltpu.VMEM((rows, rank), bf16),
            pltpu.VMEM((key_columns, rows), bf16),
            dma((SHARDS * 5,)), dma((2 * SHARDS,)), dma((3,)), dma((SHARDS,)), dma((SHARDS,)),
            dma((SHARDS,)), dma((SHARDS,)), dma((SHARDS,)), dma((SHARDS,)), dma((SHARDS,)), dma((SHARDS,)),
        ],
        compiler_params=pltpu.CompilerParams(
            collective_id=0, has_side_effects=True, vmem_limit_bytes=50 * 1024 * 1024),
        name="exchange",
    )(near, owned, tokens, cotangent, halves, adapters_t)
    grads = pl.pallas_call(
        sum_kernel,
        out_shape=jax.ShapeDtypeStruct((slot_count, rank, piece_cols), jnp.float32),
        in_specs=[smem, vmem],
        out_specs=vmem,
        compiler_params=pltpu.CompilerParams(vmem_limit_bytes=24 * 1024 * 1024),
        name="slot_sums",
    )(local, terms)
    return keys, token_gradient, jnp.swapaxes(grads, 1, 2)


def on_device(tokens, cotangent, frozen_weight, adapters, tile_job, job_slot):
    rank_width = tokens.shape[1]
    key_columns = cotangent.shape[1]
    rank = adapters.shape[2]
    slot_count = adapters.shape[0]
    row_count = adapters.shape[1]
    total_jobs = job_slot.shape[0]
    groups = lax.axis_size("grp")
    shards = lax.axis_size("seq")
    tiles_dev = tokens.shape[0] // TILE_ROWS
    group_index = lax.axis_index("grp")
    jobs = tile_job[:, 0]
    table = jnp.arange(total_jobs, dtype=jnp.int32)
    slots_all = jnp.sum(jnp.where(jobs[:, None] == table[None, :], job_slot[None, :], 0), axis=1)
    slots_all = slots_all.reshape(groups, shards, tiles_dev)
    group_slots = lax.dynamic_index_in_dim(slots_all, group_index, 0, keepdims=False)
    tile_slots = group_slots.T
    piece = lax.all_gather(frozen_weight, "seq", axis=0, tiled=True)
    forward_pass = jnp.dot(tokens, piece, preferred_element_type=jnp.float32)
    weight_update = jnp.einsum("nk,dk->nd", cotangent, piece, preferred_element_type=jnp.float32)
    owners = jnp.transpose(slots_all // slot_count, (0, 2, 1))
    local_slots = jnp.transpose(slots_all % slot_count, (0, 2, 1))
    picked = jnp.take(adapters, local_slots, axis=0)
    outgoing = jnp.where((owners == group_index)[..., None, None], picked, jnp.zeros_like(picked))
    arrived = lax.all_to_all(
        lax.all_to_all(outgoing, "grp", split_axis=0, concat_axis=0, tiled=True),
        "seq",
        split_axis=2,
        concat_axis=2,
        tiled=True,
    )
    fetched = jnp.sum(arrived.astype(jnp.float32), axis=0).astype(jnp.bfloat16)
    adapter_full = fetched.reshape(tiles_dev, shards * row_count, rank)
    down_weight = adapter_full[:, :rank_width]
    up_weight = adapter_full[:, rank_width:]
    token_tiles = tokens.reshape(tiles_dev, TILE_ROWS, rank_width)
    cot_tiles = cotangent.reshape(tiles_dev, TILE_ROWS, key_columns)
    hidden_width = jnp.einsum(
        "tnd,tdr->tnr", token_tiles, down_weight, preferred_element_type=jnp.float32
    ).astype(jnp.bfloat16)
    adapter_weights = jnp.einsum(
        "mhw,mow->mho", hidden_width, up_weight, preferred_element_type=jnp.float32
    )
    keys = (forward_pass + adapter_scale * adapter_weights.reshape(-1, key_columns)).astype(
        jnp.bfloat16
    )
    backward_pass = jnp.einsum(
        "tnk,tkr->tnr", cot_tiles, up_weight, preferred_element_type=jnp.float32
    ).astype(jnp.bfloat16)
    pass_through = jnp.einsum(
        "tnr,tdr->tnd", backward_pass, down_weight, preferred_element_type=jnp.float32
    )
    token_gradient = (weight_update + adapter_scale * pass_through.reshape(-1, rank_width)).astype(
        jnp.bfloat16
    )
    down_term = adapter_scale * jnp.einsum(
        "tnd,tnr->tdr", token_tiles, backward_pass, preferred_element_type=jnp.float32
    )
    up_term = adapter_scale * jnp.einsum(
        "tnk,tnr->tkr", cot_tiles, hidden_width, preferred_element_type=jnp.float32
    )
    terms = jnp.concatenate([down_term, up_term], axis=1).reshape(
        tiles_dev, shards, row_count, rank
    )
    incoming = lax.all_to_all(terms, "seq", split_axis=1, concat_axis=1, tiled=True)
    selector = (tile_slots.reshape(-1)[None, :] == table[:, None]).astype(jnp.float32)
    sums = jnp.dot(
        selector,
        incoming.reshape(tiles_dev * shards, row_count * rank),
        precision=lax.Precision.HIGHEST,
        preferred_element_type=jnp.float32,
    )
    owned = lax.psum_scatter(
        sums.reshape(total_jobs, row_count, rank), "grp", scatter_dimension=0, tiled=True
    )
    return (keys, token_gradient, owned)


def solution(mesh):
    placed = (
        P(("grp", "seq"), None),
        P(("grp", "seq"), None),
        P("seq", None),
        P("grp", "seq", None),
        P(),
        P(),
    )
    laid_out = mesh.shape["grp"] == 2 and mesh.shape["seq"] == SHARDS
    return jax.shard_map(
        on_block if laid_out else on_device,
        mesh=mesh,
        in_specs=placed,
        out_specs=(P(("grp", "seq"), None), P(("grp", "seq"), None), P("grp", "seq", None)),
        check_vma=False,
    )
```

```python
import functools

import jax
import jax.numpy as jnp
from jax import lax
from jax.experimental import pallas as pl
from jax.experimental.pallas import tpu as pltpu
from jax.sharding import PartitionSpec as P

TILE_ROWS = 128
MESH = pl.DeviceIdType.MESH

adapter_scale = 0.5

PLANES = 4
SHARDS = 16


def nt_dot(a, b):
    return lax.dot_general(a, b, (((1,), (1,)), ((), ())), preferred_element_type=jnp.float32)


def dot(a, b):
    return jnp.dot(a, b, preferred_element_type=jnp.float32)


def exchange_kernel(
    local_ref, owned_ref, tok_hbm, cot_hbm, w_ref, adp_hbm,
    keys_ref, tg_ref, gbuf,
    tok_ref, cot_ref, adp_ref,
    wbuf, lent, borrowed, picked, pieces, down_t, gsend, acc, back, cot_t,
    w_send, w_recv, own_sem, xa_send, xa_recv, a_send, a_recv, g_send, g_recv, xg_send, xg_recv,
):
    grp = lax.axis_index("grp")
    me = lax.axis_index("seq")
    core = me % 2
    row = (me // 2) % 2
    plane = me // 4
    rank, piece_cols = adp_ref.shape[1:]
    width = tok_ref.shape[1]
    shard_rows = width // SHARDS

    barrier = pltpu.get_barrier_semaphore()
    def greet(p, _):
        pl.semaphore_signal(barrier, inc=1, device_id=(grp, (me + p) % SHARDS), device_id_type=MESH)
        return 0
    own_copies = [
        pltpu.make_async_copy(w_ref.at[h], wbuf.at[me, h], w_recv.at[me * 2 + h]) for h in range(2)
    ]
    adp_copy = pltpu.make_async_copy(adp_hbm, adp_ref, own_sem.at[0])
    tok_copy = pltpu.make_async_copy(tok_hbm, tok_ref, own_sem.at[1])
    cot_copy = pltpu.make_async_copy(cot_hbm, cot_ref, own_sem.at[2])
    for copy in (adp_copy, *own_copies, tok_copy, cot_copy):
        copy.start()
    lax.fori_loop(1, SHARDS, greet, 0)
    pl.semaphore_signal(barrier, inc=1, device_id=(1 - grp, me), device_id_type=MESH)
    adp_copy.wait()

    def each_peer(do, away=1):
        def one(p, _):
            do((me + away * p) % SHARDS)
            return 0
        lax.fori_loop(1, SHARDS, one, 0)

    def lend(t):
        return pltpu.make_async_remote_copy(
            lent.at[t], borrowed.at[t], xa_send.at[t], xa_recv.at[t],
            device_id=(1 - grp, me), device_id_type=MESH)

    def pick_lent(t, _):
        lent[t, :, :piece_cols] = adp_ref[local_ref[(1 - grp) * SHARDS + t]]
        return 0

    edge = piece_cols // 128 * 128
    for buf in (lent, picked, gsend):
        buf[:, :, edge:] = jnp.zeros_like(buf[:, :, edge:])
    lax.fori_loop(0, SHARDS, pick_lent, 0)
    pl.semaphore_wait(barrier, SHARDS)
    each_peer(lambda t: lend(t).start())
    lend(me).start()

    def send_w(p, y, h, kind):
        s = p * 4 + y * 2 + core
        target = (
            (grp, me + 4), (grp, me - 4),
            (grp, plane * 4 + (1 - row) * 2 + core),
            (1 - grp, me),
            (grp, plane * 4 + row * 2 + 1 - core),
        )[kind]
        return pltpu.make_async_remote_copy(
            wbuf.at[s, h], wbuf.at[s, h],
            w_send.at[((p * 2 + y) * 2 + h) * 5 + kind], w_recv.at[s * 2 + h],
            device_id=target, device_id_type=MESH)

    def take_w(s, h):
        pltpu.make_async_copy(wbuf.at[s, h], wbuf.at[s, h], w_recv.at[s * 2 + h]).wait()

    def with_planes(d, do):
        for sign in (-1, 1):
            p = plane + sign * d
            ok = (d >= 0) & (p >= 0) & (p < PLANES)
            if sign > 0:
                ok = ok & (d > 0)
            pl.when(ok)(functools.partial(do, p))

    def along_planes(p, h, act):
        @pl.when((p <= plane) & (plane < PLANES - 1))
        def _():
            act(send_w(p, row, h, 0))

        @pl.when((p >= plane) & (plane > 0))
        def _():
            act(send_w(p, row, h, 1))

    def start(copy):
        copy.start()

    def finish(copy):
        copy.wait_send()

    def from_plane(p, act):
        along_planes(p, grp, act)
        act(send_w(p, row, grp, 2))
        pl.when(p != plane)(lambda: act(send_w(p, row, grp, 3)))
        act(send_w(p, row, grp, 4))
        pl.when(p == plane)(lambda: act(send_w(p, row, 1 - grp, 4)))

    def from_group(p, act):
        @pl.when(p != plane)
        def _():
            act(send_w(p, row, 1 - grp, 2))
            act(send_w(p, row, 1 - grp, 4))

        @pl.when(p == plane)
        def _():
            act(send_w(p, 1 - row, 1 - grp, 4))

    def from_row(p, act):
        pl.when(p == plane)(lambda: act(send_w(p, 1 - row, grp, 3)))
        act(send_w(p, 1 - row, grp, 4))

    def from_corner(p, act):
        pl.when(p != plane)(lambda: act(send_w(p, 1 - row, 1 - grp, 4)))

    def plane_step(p):
        take_w(p * 4 + row * 2 + core, grp)
        pl.when(p == plane)(lambda: take_w(p * 4 + row * 2 + core, 1 - grp))
        from_plane(p, start)

    def group_step(p):
        pl.when(p != plane)(lambda: take_w(p * 4 + row * 2 + core, 1 - grp))
        pl.when(p == plane)(lambda: take_w(p * 4 + (1 - row) * 2 + core, 1 - grp))
        from_group(p, start)

    def row_step(p):
        take_w(p * 4 + (1 - row) * 2 + core, grp)
        from_row(p, start)

    def corner_step(p):
        pl.when(p != plane)(lambda: take_w(p * 4 + (1 - row) * 2 + core, 1 - grp))
        from_corner(p, start)

    def core_step(p):
        for y in range(2):
            for h in range(2):
                take_w(p * 4 + y * 2 + 1 - core, h)

    def drain_step(p):
        for leaves in (from_plane, from_group, from_row, from_corner):
            leaves(p, finish)

    def compute_step(p):
        def shard(i, _):
            s = p * 4 + i
            cols = pl.ds(pl.multiple_of(s * shard_rows, shard_rows), shard_rows)
            block = wbuf[s].reshape(shard_rows, cot_ref.shape[1])
            acc[...] += dot(tok_ref[:, cols], block)
            grad = dot(block, cot_t[...]).T + adapter_scale * dot(back[...], down_t[:, cols])
            tg_ref[:, cols] = grad.astype(jnp.bfloat16)
            return 0

        lax.fori_loop(0, 4, shard, 0)

    def send_piece(k):
        return pltpu.make_async_remote_copy(
            picked.at[k], pieces.at[me], a_send.at[k], a_recv.at[me],
            device_id=(grp, k), device_id_type=MESH)

    def send_term(k):
        return pltpu.make_async_remote_copy(
            gsend.at[k], gbuf.at[grp * SHARDS + me], g_send.at[k], g_recv.at[me],
            device_id=(grp, k), device_id_type=MESH)

    def swap_term(k):
        return pltpu.make_async_remote_copy(
            gbuf.at[grp * SHARDS + k], gbuf.at[grp * SHARDS + k], xg_send.at[k], xg_recv.at[k],
            device_id=(1 - grp, me), device_id_type=MESH)

    def pick():
        def choose(t):
            lend(t).wait_recv()
            tile = grp * SHARDS + t
            picked[t, :, :piece_cols] = jnp.where(
                owned_ref[tile] == 1, adp_ref[local_ref[tile]], borrowed[t, :, :piece_cols])

        def one(t):
            choose(t)
            send_piece(t).start()

        each_peer(one)
        choose(me)
        pieces[me] = picked[me]

    def adapt():
        tok_copy.wait()
        cot_copy.wait()
        each_peer(lambda k: pltpu.make_async_copy(pieces.at[k], pieces.at[k], a_recv.at[k]).wait(), -1)
        pair = 2 * piece_cols
        for m in range(SHARDS // 2):
            down_t[:, m * pair:(m + 1) * pair] = jnp.concatenate(
                [pieces[2 * m, :, :piece_cols], pieces[2 * m + 1, :, :piece_cols]], axis=1)
        up = down_t[:, width:]
        hidden = jnp.zeros((TILE_ROWS, rank), jnp.float32)
        step = width // 4
        for q in range(4):
            t_cols = tok_ref[:, q * step:(q + 1) * step]
            d_cols = down_t[:, q * step:(q + 1) * step]
            hidden = hidden + nt_dot(t_cols, d_cols)
        hidden_t = hidden.T.astype(jnp.bfloat16)
        hidden = hidden.astype(jnp.bfloat16)
        back_wide = nt_dot(cot_ref[...], up)
        back[...] = back_wide.astype(jnp.bfloat16)
        back_t = back_wide.T.astype(jnp.bfloat16)
        cot_t[...] = cot_ref[...].T
        acc[...] = adapter_scale * dot(hidden, up)
        for m in range(SHARDS // 2):
            first, last = m * pair, (m + 1) * pair
            if last <= width:
                term = dot(back_t, tok_ref[:, first:last])
            else:
                term = jnp.concatenate(
                    [dot(back_t, tok_ref[:, first:width]), dot(hidden_t, cot_ref[:, :last - width])], axis=1)
            term = adapter_scale * term
            gsend[2 * m, :, :piece_cols] = term[:, :piece_cols].astype(jnp.bfloat16)
            gsend[2 * m + 1, :, :piece_cols] = term[:, piece_cols:].astype(jnp.bfloat16)
        each_peer(lambda k: send_term(k).start())
        gbuf[grp * SHARDS + me] = gsend[me]
        swap_term(me).start()

    def hand_on():
        def one(k):
            pltpu.make_async_copy(gbuf.at[grp * SHARDS + k], gbuf.at[grp * SHARDS + k], g_recv.at[k]).wait()
            swap_term(k).start()
        each_peer(one, -1)

    def turn(j, _):
        with_planes(j, plane_step)
        pl.when(j == 0)(pick)
        with_planes(j - 1, row_step)
        with_planes(j - 1, group_step)
        pl.when(j == 1)(adapt)
        with_planes(j - 2, corner_step)
        with_planes(j - 2, core_step)
        pl.when(j == PLANES - 1)(hand_on)
        with_planes(j - 2, compute_step)
        return 0

    lax.fori_loop(0, PLANES + 2, turn, 0)
    keys_ref[...] = acc[...].astype(jnp.bfloat16)

    def drain(d, _):
        with_planes(d, drain_step)
        return 0

    lax.fori_loop(0, PLANES, drain, 0)
    each_peer(lambda k: send_piece(k).wait_send())
    each_peer(lambda k: send_term(k).wait_send())

    def swapped(k, _):
        other = gbuf.at[(1 - grp) * SHARDS + k]
        lend(k).wait_send()
        swap_term(k).wait_send()
        pltpu.make_async_copy(other, other, xg_recv.at[k]).wait()
        return 0

    lax.fori_loop(0, SHARDS, swapped, 0)


def sum_kernel(local_ref, term_ref, out_ref):
    out_ref[...] = jnp.zeros_like(out_ref)
    slot_count = out_ref.shape[0]

    def one(t, _):
        slot = local_ref[t]

        @pl.when((slot >= 0) & (slot < slot_count))
        def _():
            out_ref[slot] += term_ref[t, :, :out_ref.shape[2]].astype(jnp.float32)

        return 0

    lax.fori_loop(0, term_ref.shape[0], one, 0)


def on_block(tokens, cotangent, frozen_weight, adapters, tile_job, job_slot):
    table = jnp.arange(job_slot.shape[0], dtype=jnp.int32)
    slots = jnp.sum(jnp.where(tile_job == table[None, :], job_slot[None, :], 0), axis=1).astype(jnp.int32)
    adapters_t = jnp.swapaxes(adapters, 1, 2)
    slot_count, rank, piece_cols = adapters_t.shape
    tiles = slots.shape[0]
    wide = -(-piece_cols // 128) * 128
    rows, width = tokens.shape
    key_columns = cotangent.shape[1]
    shard_rows = frozen_weight.shape[0]
    halves = frozen_weight.reshape(2, shard_rows // 2, key_columns)
    local = slots - lax.axis_index("grp") * slot_count
    near = jnp.clip(local, 0, slot_count - 1)
    owned = (local == near).astype(jnp.int32)
    vmem = pl.BlockSpec(memory_space=pltpu.VMEM)
    place = pl.BlockSpec(memory_space=pl.ANY)
    smem = pl.BlockSpec(memory_space=pltpu.SMEM)
    bf16 = jnp.bfloat16
    dma = pltpu.SemaphoreType.DMA
    keys, token_gradient, terms = pl.pallas_call(
        exchange_kernel,
        out_shape=(
            jax.ShapeDtypeStruct((rows, key_columns), bf16),
            jax.ShapeDtypeStruct((rows, width), bf16),
            jax.ShapeDtypeStruct((tiles, rank, wide), bf16),
        ),
        in_specs=[smem, smem, place, place, place, place],
        out_specs=(vmem, vmem, vmem),
        scratch_shapes=[
            pltpu.VMEM(tokens.shape, bf16),
            pltpu.VMEM(cotangent.shape, bf16),
            pltpu.VMEM(adapters_t.shape, bf16),
            pltpu.VMEM((SHARDS, 2, shard_rows // 2, key_columns), bf16),
            pltpu.VMEM((SHARDS, rank, wide), bf16),
            pltpu.VMEM((SHARDS, rank, wide), bf16),
            pltpu.VMEM((SHARDS, rank, wide), bf16),
            pltpu.VMEM((SHARDS, rank, wide), bf16),
            pltpu.VMEM((rank, SHARDS * piece_cols), bf16),
            pltpu.VMEM((SHARDS, rank, wide), bf16),
            pltpu.VMEM((rows, key_columns), jnp.float32),
            pltpu.VMEM((rows, rank), bf16),
            pltpu.VMEM((key_columns, rows), bf16),
            dma((SHARDS * 5,)), dma((2 * SHARDS,)), dma((3,)), dma((SHARDS,)), dma((SHARDS,)),
            dma((SHARDS,)), dma((SHARDS,)), dma((SHARDS,)), dma((SHARDS,)), dma((SHARDS,)), dma((SHARDS,)),
        ],
        compiler_params=pltpu.CompilerParams(
            collective_id=0, has_side_effects=True, vmem_limit_bytes=60 * 1024 * 1024),
        name="exchange",
    )(near, owned, tokens, cotangent, halves, adapters_t)
    grads = pl.pallas_call(
        sum_kernel,
        out_shape=jax.ShapeDtypeStruct((slot_count, rank, piece_cols), jnp.float32),
        in_specs=[smem, vmem],
        out_specs=vmem,
        compiler_params=pltpu.CompilerParams(vmem_limit_bytes=24 * 1024 * 1024),
        name="slot_sums",
    )(local, terms)
    return keys, token_gradient, jnp.swapaxes(grads, 1, 2)


def on_device(tokens, cotangent, frozen_weight, adapters, tile_job, job_slot):
    rank_width = tokens.shape[1]
    key_columns = cotangent.shape[1]
    rank = adapters.shape[2]
    slot_count = adapters.shape[0]
    row_count = adapters.shape[1]
    total_jobs = job_slot.shape[0]
    groups = lax.axis_size("grp")
    shards = lax.axis_size("seq")
    tiles_dev = tokens.shape[0] // TILE_ROWS
    group_index = lax.axis_index("grp")
    jobs = tile_job[:, 0]
    table = jnp.arange(total_jobs, dtype=jnp.int32)
    slots_all = jnp.sum(jnp.where(jobs[:, None] == table[None, :], job_slot[None, :], 0), axis=1)
    slots_all = slots_all.reshape(groups, shards, tiles_dev)
    group_slots = lax.dynamic_index_in_dim(slots_all, group_index, 0, keepdims=False)
    tile_slots = group_slots.T
    piece = lax.all_gather(frozen_weight, "seq", axis=0, tiled=True)
    forward_pass = jnp.dot(tokens, piece, preferred_element_type=jnp.float32)
    weight_update = jnp.einsum("nk,dk->nd", cotangent, piece, preferred_element_type=jnp.float32)
    owners = jnp.transpose(slots_all // slot_count, (0, 2, 1))
    local_slots = jnp.transpose(slots_all % slot_count, (0, 2, 1))
    picked = jnp.take(adapters, local_slots, axis=0)
    outgoing = jnp.where((owners == group_index)[..., None, None], picked, jnp.zeros_like(picked))
    arrived = lax.all_to_all(
        lax.all_to_all(outgoing, "grp", split_axis=0, concat_axis=0, tiled=True),
        "seq",
        split_axis=2,
        concat_axis=2,
        tiled=True,
    )
    fetched = jnp.sum(arrived.astype(jnp.float32), axis=0).astype(jnp.bfloat16)
    adapter_full = fetched.reshape(tiles_dev, shards * row_count, rank)
    down_weight = adapter_full[:, :rank_width]
    up_weight = adapter_full[:, rank_width:]
    token_tiles = tokens.reshape(tiles_dev, TILE_ROWS, rank_width)
    cot_tiles = cotangent.reshape(tiles_dev, TILE_ROWS, key_columns)
    hidden_width = jnp.einsum(
        "tnd,tdr->tnr", token_tiles, down_weight, preferred_element_type=jnp.float32
    ).astype(jnp.bfloat16)
    adapter_weights = jnp.einsum(
        "mhw,mow->mho", hidden_width, up_weight, preferred_element_type=jnp.float32
    )
    keys = (forward_pass + adapter_scale * adapter_weights.reshape(-1, key_columns)).astype(
        jnp.bfloat16
    )
    backward_pass = jnp.einsum(
        "tnk,tkr->tnr", cot_tiles, up_weight, preferred_element_type=jnp.float32
    ).astype(jnp.bfloat16)
    pass_through = jnp.einsum(
        "tnr,tdr->tnd", backward_pass, down_weight, preferred_element_type=jnp.float32
    )
    token_gradient = (weight_update + adapter_scale * pass_through.reshape(-1, rank_width)).astype(
        jnp.bfloat16
    )
    down_term = adapter_scale * jnp.einsum(
        "tnd,tnr->tdr", token_tiles, backward_pass, preferred_element_type=jnp.float32
    )
    up_term = adapter_scale * jnp.einsum(
        "tnk,tnr->tkr", cot_tiles, hidden_width, preferred_element_type=jnp.float32
    )
    terms = jnp.concatenate([down_term, up_term], axis=1).reshape(
        tiles_dev, shards, row_count, rank
    )
    incoming = lax.all_to_all(terms, "seq", split_axis=1, concat_axis=1, tiled=True)
    selector = (tile_slots.reshape(-1)[None, :] == table[:, None]).astype(jnp.float32)
    sums = jnp.dot(
        selector,
        incoming.reshape(tiles_dev * shards, row_count * rank),
        precision=lax.Precision.HIGHEST,
        preferred_element_type=jnp.float32,
    )
    owned = lax.psum_scatter(
        sums.reshape(total_jobs, row_count, rank), "grp", scatter_dimension=0, tiled=True
    )
    return (keys, token_gradient, owned)


def solution(mesh):
    placed = (
        P(("grp", "seq"), None),
        P(("grp", "seq"), None),
        P("seq", None),
        P("grp", "seq", None),
        P(),
        P(),
    )
    laid_out = mesh.shape["grp"] == 2 and mesh.shape["seq"] == SHARDS
    return jax.shard_map(
        on_block if laid_out else on_device,
        mesh=mesh,
        in_specs=placed,
        out_specs=(P(("grp", "seq"), None), P(("grp", "seq"), None), P("grp", "seq", None)),
        check_vma=False,
    )
```

```python
import functools

import jax
import jax.numpy as jnp
from jax import lax
from jax.experimental import pallas as pl
from jax.experimental.pallas import tpu as pltpu
from jax.sharding import PartitionSpec as P

TILE_ROWS = 128
MESH = pl.DeviceIdType.MESH

adapter_scale = 0.5

PLANES = 4
SHARDS = 16


def nt_dot(a, b):
    return lax.dot_general(a, b, (((1,), (1,)), ((), ())), preferred_element_type=jnp.float32)


def dot(a, b):
    return jnp.dot(a, b, preferred_element_type=jnp.float32)


def exchange_kernel(
    local_ref, owned_ref, tok_hbm, cot_hbm, w_ref, adp_hbm,
    keys_ref, tg_ref, gbuf,
    tok_ref, cot_ref, adp_ref,
    wbuf, lent, borrowed, picked, pieces, down_t, gsend, acc, back, cot_t,
    w_send, w_recv, own_sem, xa_send, xa_recv, a_send, a_recv, g_send, g_recv, xg_send, xg_recv,
):
    grp = lax.axis_index("grp")
    me = lax.axis_index("seq")
    core = me % 2
    row = (me // 2) % 2
    plane = me // 4
    rank, piece_cols = adp_ref.shape[1:]
    width = tok_ref.shape[1]
    shard_rows = width // SHARDS

    barrier = pltpu.get_barrier_semaphore()
    def greet(p, _):
        pl.semaphore_signal(barrier, inc=1, device_id=(grp, (me + p) % SHARDS), device_id_type=MESH)
        return 0
    own_copies = [
        pltpu.make_async_copy(w_ref.at[h], wbuf.at[me, h], w_recv.at[me * 2 + h]) for h in range(2)
    ]
    adp_copy = pltpu.make_async_copy(adp_hbm, adp_ref, own_sem.at[0])
    tok_copy = pltpu.make_async_copy(tok_hbm, tok_ref, own_sem.at[1])
    cot_copy = pltpu.make_async_copy(cot_hbm, cot_ref, own_sem.at[2])
    for copy in (adp_copy, *own_copies, tok_copy, cot_copy):
        copy.start()
    lax.fori_loop(1, SHARDS, greet, 0)
    pl.semaphore_signal(barrier, inc=1, device_id=(1 - grp, me), device_id_type=MESH)
    adp_copy.wait()

    def each_peer(do, away=1, first=1, last=SHARDS):
        def one(p, _):
            do((me + away * p) % SHARDS)
            return 0
        lax.fori_loop(first, last, one, 0)

    def lend(t):
        return pltpu.make_async_remote_copy(
            lent.at[t], borrowed.at[t], xa_send.at[t], xa_recv.at[t],
            device_id=(1 - grp, me), device_id_type=MESH)

    def pick_lent(t, _):
        lent[t, :, :piece_cols] = adp_ref[local_ref[(1 - grp) * SHARDS + t]]
        return 0

    edge = piece_cols // 128 * 128
    for buf in (lent, picked, gsend):
        buf[:, :, edge:] = jnp.zeros_like(buf[:, :, edge:])
    lax.fori_loop(0, SHARDS, pick_lent, 0)
    pl.semaphore_wait(barrier, SHARDS)
    each_peer(lambda t: lend(t).start())
    lend(me).start()

    def send_w(p, y, h, kind):
        s = p * 4 + y * 2 + core
        target = (
            (grp, me + 4), (grp, me - 4),
            (grp, plane * 4 + (1 - row) * 2 + core),
            (1 - grp, me),
            (grp, plane * 4 + row * 2 + 1 - core),
        )[kind]
        return pltpu.make_async_remote_copy(
            wbuf.at[s, h], wbuf.at[s, h],
            w_send.at[((p * 2 + y) * 2 + h) * 5 + kind], w_recv.at[s * 2 + h],
            device_id=target, device_id_type=MESH)

    def take_w(s, h):
        pltpu.make_async_copy(wbuf.at[s, h], wbuf.at[s, h], w_recv.at[s * 2 + h]).wait()

    def with_planes(d, do):
        for sign in (-1, 1):
            p = plane + sign * d
            ok = (d >= 0) & (p >= 0) & (p < PLANES)
            if sign > 0:
                ok = ok & (d > 0)
            pl.when(ok)(functools.partial(do, p))

    def along_planes(p, h, act):
        @pl.when((p <= plane) & (plane < PLANES - 1))
        def _():
            act(send_w(p, row, h, 0))

        @pl.when((p >= plane) & (plane > 0))
        def _():
            act(send_w(p, row, h, 1))

    def start(copy):
        copy.start()

    def finish(copy):
        copy.wait_send()

    def whole(p):
        return (p == plane) | (core == 0)

    def from_plane(p, act):
        along_planes(p, grp, act)
        pl.when(core == 0)(lambda: along_planes(p, 1 - grp, act))
        act(send_w(p, row, grp, 2))
        pl.when(~whole(p))(lambda: act(send_w(p, row, grp, 3)))
        act(send_w(p, row, grp, 4))
        pl.when(whole(p))(lambda: act(send_w(p, row, 1 - grp, 4)))

    def from_group(p, act):
        @pl.when(~whole(p))
        def _():
            act(send_w(p, row, 1 - grp, 2))
            act(send_w(p, row, 1 - grp, 4))

        @pl.when(whole(p))
        def _():
            act(send_w(p, 1 - row, 1 - grp, 4))

    def from_row(p, act):
        pl.when(whole(p))(lambda: act(send_w(p, 1 - row, grp, 3)))
        act(send_w(p, 1 - row, grp, 4))

    def from_corner(p, act):
        pl.when(~whole(p))(lambda: act(send_w(p, 1 - row, 1 - grp, 4)))

    def plane_step(p):
        take_w(p * 4 + row * 2 + core, grp)
        pl.when(whole(p))(lambda: take_w(p * 4 + row * 2 + core, 1 - grp))
        from_plane(p, start)

    def group_step(p):
        pl.when(~whole(p))(lambda: take_w(p * 4 + row * 2 + core, 1 - grp))
        pl.when(whole(p))(lambda: take_w(p * 4 + (1 - row) * 2 + core, 1 - grp))
        from_group(p, start)

    def row_step(p):
        take_w(p * 4 + (1 - row) * 2 + core, grp)
        from_row(p, start)

    def corner_step(p):
        pl.when(~whole(p))(lambda: take_w(p * 4 + (1 - row) * 2 + core, 1 - grp))
        from_corner(p, start)

    def core_step(p):
        for y in range(2):
            for h in range(2):
                take_w(p * 4 + y * 2 + 1 - core, h)

    def drain_step(p):
        for leaves in (from_plane, from_group, from_row, from_corner):
            leaves(p, finish)

    def compute_step(p):
        def shard(i, _):
            s = p * 4 + i
            cols = pl.ds(pl.multiple_of(s * shard_rows, shard_rows), shard_rows)
            block = wbuf[s].reshape(shard_rows, cot_ref.shape[1])
            acc[...] += dot(tok_ref[:, cols], block)
            grad = dot(block, cot_t[...]).T + adapter_scale * dot(back[...], down_t[:, cols])
            tg_ref[:, cols] = grad.astype(jnp.bfloat16)
            return 0

        lax.fori_loop(0, 4, shard, 0)

    def send_piece(k):
        return pltpu.make_async_remote_copy(
            picked.at[k], pieces.at[me], a_send.at[k], a_recv.at[me],
            device_id=(grp, k), device_id_type=MESH)

    def send_term(k):
        return pltpu.make_async_remote_copy(
            gsend.at[k], gbuf.at[grp * SHARDS + me], g_send.at[k], g_recv.at[me],
            device_id=(grp, k), device_id_type=MESH)

    def swap_term(k):
        return pltpu.make_async_remote_copy(
            gbuf.at[grp * SHARDS + k], gbuf.at[grp * SHARDS + k], xg_send.at[k], xg_recv.at[k],
            device_id=(1 - grp, me), device_id_type=MESH)

    def pick(first, last):
        def choose(t):
            lend(t).wait_recv()
            tile = grp * SHARDS + t
            picked[t, :, :piece_cols] = jnp.where(
                owned_ref[tile] == 1, adp_ref[local_ref[tile]], borrowed[t, :, :piece_cols])

        def one(t):
            choose(t)
            send_piece(t).start()

        each_peer(one, 1, first, last)

        @pl.when(last == SHARDS)
        def _():
            choose(me)
            pieces[me] = picked[me]

    def adapt():
        tok_copy.wait()
        cot_copy.wait()
        each_peer(lambda k: pltpu.make_async_copy(pieces.at[k], pieces.at[k], a_recv.at[k]).wait(), -1)
        pair = 2 * piece_cols
        for m in range(SHARDS // 2):
            down_t[:, m * pair:(m + 1) * pair] = jnp.concatenate(
                [pieces[2 * m, :, :piece_cols], pieces[2 * m + 1, :, :piece_cols]], axis=1)
        up = down_t[:, width:]
        hidden = jnp.zeros((TILE_ROWS, rank), jnp.float32)
        step = width // 4
        for q in range(4):
            t_cols = tok_ref[:, q * step:(q + 1) * step]
            d_cols = down_t[:, q * step:(q + 1) * step]
            hidden = hidden + nt_dot(t_cols, d_cols)
        hidden_t = hidden.T.astype(jnp.bfloat16)
        hidden = hidden.astype(jnp.bfloat16)
        back_wide = nt_dot(cot_ref[...], up)
        back[...] = back_wide.astype(jnp.bfloat16)
        back_t = back_wide.T.astype(jnp.bfloat16)
        cot_t[...] = cot_ref[...].T
        acc[...] = adapter_scale * dot(hidden, up)
        for m in range(SHARDS // 2):
            first, last = m * pair, (m + 1) * pair
            if last <= width:
                term = dot(back_t, tok_ref[:, first:last])
            else:
                term = jnp.concatenate(
                    [dot(back_t, tok_ref[:, first:width]), dot(hidden_t, cot_ref[:, :last - width])], axis=1)
            term = adapter_scale * term
            gsend[2 * m, :, :piece_cols] = term[:, :piece_cols].astype(jnp.bfloat16)
            gsend[2 * m + 1, :, :piece_cols] = term[:, piece_cols:].astype(jnp.bfloat16)
        each_peer(lambda k: send_term(k).start())
        gbuf[grp * SHARDS + me] = gsend[me]
        swap_term(me).start()

    def hand_on(first, last):
        def one(k):
            pltpu.make_async_copy(gbuf.at[grp * SHARDS + k], gbuf.at[grp * SHARDS + k], g_recv.at[k]).wait()
            swap_term(k).start()
        each_peer(one, -1, first, last)

    middle = SHARDS // 2

    def turn(j, _):
        with_planes(j, plane_step)
        with_planes(j - 1, row_step)
        pl.when(j < 2)(lambda: pick(1 + j * (middle - 1), middle + j * middle))
        with_planes(j - 1, group_step)
        pl.when(j == 2)(adapt)
        with_planes(j - 2, corner_step)
        with_planes(j - 2, core_step)
        pl.when((j == 3) | (j == 4))(
            lambda: hand_on(1 + (j - 3) * (middle - 1), middle + (j - 3) * middle))
        with_planes(j - 2, compute_step)
        return 0

    lax.fori_loop(0, PLANES + 2, turn, 0)
    keys_ref[...] = acc[...].astype(jnp.bfloat16)

    def drain(d, _):
        with_planes(d, drain_step)
        return 0

    lax.fori_loop(0, PLANES, drain, 0)
    each_peer(lambda k: send_piece(k).wait_send())
    each_peer(lambda k: send_term(k).wait_send())

    def swapped(k, _):
        other = gbuf.at[(1 - grp) * SHARDS + k]
        lend(k).wait_send()
        swap_term(k).wait_send()
        pltpu.make_async_copy(other, other, xg_recv.at[k]).wait()
        return 0

    lax.fori_loop(0, SHARDS, swapped, 0)


def sum_kernel(local_ref, term_ref, out_ref):
    out_ref[...] = jnp.zeros_like(out_ref)
    slot_count = out_ref.shape[0]

    def one(t, _):
        slot = local_ref[t]

        @pl.when((slot >= 0) & (slot < slot_count))
        def _():
            out_ref[slot] += term_ref[t, :, :out_ref.shape[2]].astype(jnp.float32)

        return 0

    lax.fori_loop(0, term_ref.shape[0], one, 0)


def on_block(tokens, cotangent, frozen_weight, adapters, tile_job, job_slot):
    table = jnp.arange(job_slot.shape[0], dtype=jnp.int32)
    slots = jnp.sum(jnp.where(tile_job == table[None, :], job_slot[None, :], 0), axis=1).astype(jnp.int32)
    adapters_t = jnp.swapaxes(adapters, 1, 2)
    slot_count, rank, piece_cols = adapters_t.shape
    tiles = slots.shape[0]
    wide = -(-piece_cols // 128) * 128
    rows, width = tokens.shape
    key_columns = cotangent.shape[1]
    shard_rows = frozen_weight.shape[0]
    halves = frozen_weight.reshape(2, shard_rows // 2, key_columns)
    local = slots - lax.axis_index("grp") * slot_count
    near = jnp.clip(local, 0, slot_count - 1)
    owned = (local == near).astype(jnp.int32)
    vmem = pl.BlockSpec(memory_space=pltpu.VMEM)
    place = pl.BlockSpec(memory_space=pl.ANY)
    smem = pl.BlockSpec(memory_space=pltpu.SMEM)
    bf16 = jnp.bfloat16
    dma = pltpu.SemaphoreType.DMA
    keys, token_gradient, terms = pl.pallas_call(
        exchange_kernel,
        out_shape=(
            jax.ShapeDtypeStruct((rows, key_columns), bf16),
            jax.ShapeDtypeStruct((rows, width), bf16),
            jax.ShapeDtypeStruct((tiles, rank, wide), bf16),
        ),
        in_specs=[smem, smem, place, place, place, place],
        out_specs=(vmem, vmem, vmem),
        scratch_shapes=[
            pltpu.VMEM(tokens.shape, bf16),
            pltpu.VMEM(cotangent.shape, bf16),
            pltpu.VMEM(adapters_t.shape, bf16),
            pltpu.VMEM((SHARDS, 2, shard_rows // 2, key_columns), bf16),
            pltpu.VMEM((SHARDS, rank, wide), bf16),
            pltpu.VMEM((SHARDS, rank, wide), bf16),
            pltpu.VMEM((SHARDS, rank, wide), bf16),
            pltpu.VMEM((SHARDS, rank, wide), bf16),
            pltpu.VMEM((rank, SHARDS * piece_cols), bf16),
            pltpu.VMEM((SHARDS, rank, wide), bf16),
            pltpu.VMEM((rows, key_columns), jnp.float32),
            pltpu.VMEM((rows, rank), bf16),
            pltpu.VMEM((key_columns, rows), bf16),
            dma((SHARDS * 5,)), dma((2 * SHARDS,)), dma((3,)), dma((SHARDS,)), dma((SHARDS,)),
            dma((SHARDS,)), dma((SHARDS,)), dma((SHARDS,)), dma((SHARDS,)), dma((SHARDS,)), dma((SHARDS,)),
        ],
        compiler_params=pltpu.CompilerParams(
            collective_id=0, has_side_effects=True, vmem_limit_bytes=60 * 1024 * 1024),
        name="exchange",
    )(near, owned, tokens, cotangent, halves, adapters_t)
    grads = pl.pallas_call(
        sum_kernel,
        out_shape=jax.ShapeDtypeStruct((slot_count, rank, piece_cols), jnp.float32),
        in_specs=[smem, vmem],
        out_specs=vmem,
        compiler_params=pltpu.CompilerParams(vmem_limit_bytes=24 * 1024 * 1024),
        name="slot_sums",
    )(local, terms)
    return keys, token_gradient, jnp.swapaxes(grads, 1, 2)


def on_device(tokens, cotangent, frozen_weight, adapters, tile_job, job_slot):
    rank_width = tokens.shape[1]
    key_columns = cotangent.shape[1]
    rank = adapters.shape[2]
    slot_count = adapters.shape[0]
    row_count = adapters.shape[1]
    total_jobs = job_slot.shape[0]
    groups = lax.axis_size("grp")
    shards = lax.axis_size("seq")
    tiles_dev = tokens.shape[0] // TILE_ROWS
    group_index = lax.axis_index("grp")
    jobs = tile_job[:, 0]
    table = jnp.arange(total_jobs, dtype=jnp.int32)
    slots_all = jnp.sum(jnp.where(jobs[:, None] == table[None, :], job_slot[None, :], 0), axis=1)
    slots_all = slots_all.reshape(groups, shards, tiles_dev)
    group_slots = lax.dynamic_index_in_dim(slots_all, group_index, 0, keepdims=False)
    tile_slots = group_slots.T
    piece = lax.all_gather(frozen_weight, "seq", axis=0, tiled=True)
    forward_pass = jnp.dot(tokens, piece, preferred_element_type=jnp.float32)
    weight_update = jnp.einsum("nk,dk->nd", cotangent, piece, preferred_element_type=jnp.float32)
    owners = jnp.transpose(slots_all // slot_count, (0, 2, 1))
    local_slots = jnp.transpose(slots_all % slot_count, (0, 2, 1))
    picked = jnp.take(adapters, local_slots, axis=0)
    outgoing = jnp.where((owners == group_index)[..., None, None], picked, jnp.zeros_like(picked))
    arrived = lax.all_to_all(
        lax.all_to_all(outgoing, "grp", split_axis=0, concat_axis=0, tiled=True),
        "seq",
        split_axis=2,
        concat_axis=2,
        tiled=True,
    )
    fetched = jnp.sum(arrived.astype(jnp.float32), axis=0).astype(jnp.bfloat16)
    adapter_full = fetched.reshape(tiles_dev, shards * row_count, rank)
    down_weight = adapter_full[:, :rank_width]
    up_weight = adapter_full[:, rank_width:]
    token_tiles = tokens.reshape(tiles_dev, TILE_ROWS, rank_width)
    cot_tiles = cotangent.reshape(tiles_dev, TILE_ROWS, key_columns)
    hidden_width = jnp.einsum(
        "tnd,tdr->tnr", token_tiles, down_weight, preferred_element_type=jnp.float32
    ).astype(jnp.bfloat16)
    adapter_weights = jnp.einsum(
        "mhw,mow->mho", hidden_width, up_weight, preferred_element_type=jnp.float32
    )
    keys = (forward_pass + adapter_scale * adapter_weights.reshape(-1, key_columns)).astype(
        jnp.bfloat16
    )
    backward_pass = jnp.einsum(
        "tnk,tkr->tnr", cot_tiles, up_weight, preferred_element_type=jnp.float32
    ).astype(jnp.bfloat16)
    pass_through = jnp.einsum(
        "tnr,tdr->tnd", backward_pass, down_weight, preferred_element_type=jnp.float32
    )
    token_gradient = (weight_update + adapter_scale * pass_through.reshape(-1, rank_width)).astype(
        jnp.bfloat16
    )
    down_term = adapter_scale * jnp.einsum(
        "tnd,tnr->tdr", token_tiles, backward_pass, preferred_element_type=jnp.float32
    )
    up_term = adapter_scale * jnp.einsum(
        "tnk,tnr->tkr", cot_tiles, hidden_width, preferred_element_type=jnp.float32
    )
    terms = jnp.concatenate([down_term, up_term], axis=1).reshape(
        tiles_dev, shards, row_count, rank
    )
    incoming = lax.all_to_all(terms, "seq", split_axis=1, concat_axis=1, tiled=True)
    selector = (tile_slots.reshape(-1)[None, :] == table[:, None]).astype(jnp.float32)
    sums = jnp.dot(
        selector,
        incoming.reshape(tiles_dev * shards, row_count * rank),
        precision=lax.Precision.HIGHEST,
        preferred_element_type=jnp.float32,
    )
    owned = lax.psum_scatter(
        sums.reshape(total_jobs, row_count, rank), "grp", scatter_dimension=0, tiled=True
    )
    return (keys, token_gradient, owned)


def solution(mesh):
    placed = (
        P(("grp", "seq"), None),
        P(("grp", "seq"), None),
        P("seq", None),
        P("grp", "seq", None),
        P(),
        P(),
    )
    laid_out = mesh.shape["grp"] == 2 and mesh.shape["seq"] == SHARDS
    return jax.shard_map(
        on_block if laid_out else on_device,
        mesh=mesh,
        in_specs=placed,
        out_specs=(P(("grp", "seq"), None), P(("grp", "seq"), None), P("grp", "seq", None)),
        check_vma=False,
    )
```

```python
import functools

import jax
import jax.numpy as jnp
from jax import lax
from jax.experimental import pallas as pl
from jax.experimental.pallas import tpu as pltpu
from jax.sharding import PartitionSpec as P

TILE_ROWS = 128
MESH = pl.DeviceIdType.MESH

adapter_scale = 0.5

PLANES = 4
SHARDS = 16


def nt_dot(a, b):
    return lax.dot_general(a, b, (((1,), (1,)), ((), ())), preferred_element_type=jnp.float32)


def dot(a, b):
    return jnp.dot(a, b, preferred_element_type=jnp.float32)


def exchange_kernel(
    slots_ref, tok_hbm, cot_hbm, w_ref, adp_hbm,
    keys_ref, tg_ref, gbuf,
    tok_ref, cot_ref, adp_ref,
    wbuf, lent, borrowed, picked, pieces, down_t, gsend, acc, back, cot_t,
    w_send, w_recv, own_sem, xa_send, xa_recv, a_send, a_recv, g_send, g_recv, xg_send, xg_recv,
):
    grp = lax.axis_index("grp")
    me = lax.axis_index("seq")
    core = me % 2
    row = (me // 2) % 2
    plane = me // 4
    slot_count, rank, piece_cols = adp_ref.shape
    width = tok_ref.shape[1]
    shard_rows = width // SHARDS

    barrier = pltpu.get_barrier_semaphore()
    def greet(p, _):
        pl.semaphore_signal(barrier, inc=1, device_id=(grp, (me + p) % SHARDS), device_id_type=MESH)
        return 0
    own_copies = [
        pltpu.make_async_copy(w_ref.at[h], wbuf.at[me, h], w_recv.at[me * 2 + h]) for h in range(2)
    ]
    adp_copy = pltpu.make_async_copy(adp_hbm, adp_ref, own_sem.at[0])
    tok_copy = pltpu.make_async_copy(tok_hbm, tok_ref, own_sem.at[1])
    cot_copy = pltpu.make_async_copy(cot_hbm, cot_ref, own_sem.at[2])
    for copy in (adp_copy, *own_copies, tok_copy, cot_copy):
        copy.start()
    lax.fori_loop(1, SHARDS, greet, 0)
    pl.semaphore_signal(barrier, inc=1, device_id=(1 - grp, me), device_id_type=MESH)
    adp_copy.wait()

    def each_peer(do, away=1, first=1, last=SHARDS):
        def one(p, _):
            do((me + away * p) % SHARDS)
            return 0
        lax.fori_loop(first, last, one, 0)

    def lend(t):
        return pltpu.make_async_remote_copy(
            lent.at[t], borrowed.at[t], xa_send.at[t], xa_recv.at[t],
            device_id=(1 - grp, me), device_id_type=MESH)

    def local_of(tile):
        local = slots_ref[tile] - grp * slot_count
        held = jnp.minimum(jnp.maximum(local, 0), slot_count - 1)
        return local == held, held

    def pick_lent(t, _):
        lent[t, :, :piece_cols] = adp_ref[local_of((1 - grp) * SHARDS + t)[1]]
        return 0

    edge = piece_cols // 128 * 128
    for buf in (lent, picked, gsend):
        buf[:, :, edge:] = jnp.zeros_like(buf[:, :, edge:])
    lax.fori_loop(0, SHARDS, pick_lent, 0)
    pl.semaphore_wait(barrier, SHARDS)
    each_peer(lambda t: lend(t).start())
    lend(me).start()

    def send_w(p, y, h, kind):
        s = p * 4 + y * 2 + core
        target = (
            (grp, me + 4), (grp, me - 4),
            (grp, plane * 4 + (1 - row) * 2 + core),
            (1 - grp, me),
            (grp, plane * 4 + row * 2 + 1 - core),
        )[kind]
        return pltpu.make_async_remote_copy(
            wbuf.at[s, h], wbuf.at[s, h],
            w_send.at[((p * 2 + y) * 2 + h) * 5 + kind], w_recv.at[s * 2 + h],
            device_id=target, device_id_type=MESH)

    def take_w(s, h):
        pltpu.make_async_copy(wbuf.at[s, h], wbuf.at[s, h], w_recv.at[s * 2 + h]).wait()

    def with_planes(d, do):
        for sign in (-1, 1):
            p = plane + sign * d
            ok = (d >= 0) & (p >= 0) & (p < PLANES)
            if sign > 0:
                ok = ok & (d > 0)
            pl.when(ok)(functools.partial(do, p))

    def along_planes(p, h, act, reach=PLANES):
        @pl.when((p <= plane) & (plane < PLANES - 1) & (plane + 1 - p <= reach))
        def _():
            act(send_w(p, row, h, 0))

        @pl.when((p >= plane) & (plane > 0) & (p - plane + 1 <= reach))
        def _():
            act(send_w(p, row, h, 1))

    def start(copy):
        copy.start()

    def finish(copy):
        copy.wait_send()

    near = PLANES - 2

    def whole(p):
        return (p == plane) | ((core == 0) & (p - plane <= near) & (plane - p <= near))

    def from_plane(p, act):
        along_planes(p, grp, act)
        pl.when(core == 0)(lambda: along_planes(p, 1 - grp, act, near))
        act(send_w(p, row, grp, 2))
        pl.when(~whole(p))(lambda: act(send_w(p, row, grp, 3)))
        act(send_w(p, row, grp, 4))
        pl.when(whole(p))(lambda: act(send_w(p, row, 1 - grp, 4)))

    def from_group(p, act):
        @pl.when(~whole(p))
        def _():
            act(send_w(p, row, 1 - grp, 2))
            act(send_w(p, row, 1 - grp, 4))

        @pl.when(whole(p))
        def _():
            act(send_w(p, 1 - row, 1 - grp, 4))

    def from_row(p, act):
        pl.when(whole(p))(lambda: act(send_w(p, 1 - row, grp, 3)))
        act(send_w(p, 1 - row, grp, 4))

    def from_corner(p, act):
        pl.when(~whole(p))(lambda: act(send_w(p, 1 - row, 1 - grp, 4)))

    def plane_step(p):
        take_w(p * 4 + row * 2 + core, grp)
        pl.when(whole(p))(lambda: take_w(p * 4 + row * 2 + core, 1 - grp))
        from_plane(p, start)

    def group_step(p):
        pl.when(~whole(p))(lambda: take_w(p * 4 + row * 2 + core, 1 - grp))
        pl.when(whole(p))(lambda: take_w(p * 4 + (1 - row) * 2 + core, 1 - grp))
        from_group(p, start)

    def row_step(p):
        take_w(p * 4 + (1 - row) * 2 + core, grp)
        from_row(p, start)

    def corner_step(p):
        pl.when(~whole(p))(lambda: take_w(p * 4 + (1 - row) * 2 + core, 1 - grp))
        from_corner(p, start)

    def core_step(p):
        for y in range(2):
            for h in range(2):
                take_w(p * 4 + y * 2 + 1 - core, h)

    def drain_step(p):
        for leaves in (from_plane, from_group, from_row, from_corner):
            leaves(p, finish)

    def compute_step(p):
        def shard(i, _):
            s = p * 4 + i
            cols = pl.ds(pl.multiple_of(s * shard_rows, shard_rows), shard_rows)
            block = wbuf[s].reshape(shard_rows, cot_ref.shape[1])
            acc[...] += dot(tok_ref[:, cols], block)
            grad = dot(block, cot_t[...]).T + adapter_scale * dot(back[...], down_t[:, cols])
            tg_ref[:, cols] = grad.astype(jnp.bfloat16)
            return 0

        lax.fori_loop(0, 4, shard, 0)

    def send_piece(k):
        return pltpu.make_async_remote_copy(
            picked.at[k], pieces.at[me], a_send.at[k], a_recv.at[me],
            device_id=(grp, k), device_id_type=MESH)

    def send_term(k):
        return pltpu.make_async_remote_copy(
            gsend.at[k], gbuf.at[grp * SHARDS + me], g_send.at[k], g_recv.at[me],
            device_id=(grp, k), device_id_type=MESH)

    def swap_term(k):
        return pltpu.make_async_remote_copy(
            gbuf.at[grp * SHARDS + k], gbuf.at[grp * SHARDS + k], xg_send.at[k], xg_recv.at[k],
            device_id=(1 - grp, me), device_id_type=MESH)

    def pick(first, last):
        def choose(t):
            lend(t).wait_recv()
            owned, held = local_of(grp * SHARDS + t)
            picked[t, :, :piece_cols] = jnp.where(
                owned, adp_ref[held], borrowed[t, :, :piece_cols])

        def one(t):
            choose(t)
            send_piece(t).start()

        each_peer(one, 1, first, last)

        @pl.when(last == SHARDS)
        def _():
            choose(me)
            pieces[me] = picked[me]

    def adapt():
        tok_copy.wait()
        cot_copy.wait()
        each_peer(lambda k: pltpu.make_async_copy(pieces.at[k], pieces.at[k], a_recv.at[k]).wait(), -1)
        pair = 2 * piece_cols
        for m in range(SHARDS // 2):
            down_t[:, m * pair:(m + 1) * pair] = jnp.concatenate(
                [pieces[2 * m, :, :piece_cols], pieces[2 * m + 1, :, :piece_cols]], axis=1)
        up = down_t[:, width:]
        hidden = jnp.zeros((TILE_ROWS, rank), jnp.float32)
        step = width // 4
        for q in range(4):
            t_cols = tok_ref[:, q * step:(q + 1) * step]
            d_cols = down_t[:, q * step:(q + 1) * step]
            hidden = hidden + nt_dot(t_cols, d_cols)
        hidden_t = hidden.T.astype(jnp.bfloat16)
        hidden = hidden.astype(jnp.bfloat16)
        back_wide = nt_dot(cot_ref[...], up)
        back[...] = back_wide.astype(jnp.bfloat16)
        back_t = back_wide.T.astype(jnp.bfloat16)
        cot_t[...] = cot_ref[...].T
        acc[...] = adapter_scale * dot(hidden, up)
        for m in range(SHARDS // 2):
            first, last = m * pair, (m + 1) * pair
            if last <= width:
                term = dot(back_t, tok_ref[:, first:last])
            else:
                term = jnp.concatenate(
                    [dot(back_t, tok_ref[:, first:width]), dot(hidden_t, cot_ref[:, :last - width])], axis=1)
            term = adapter_scale * term
            gsend[2 * m, :, :piece_cols] = term[:, :piece_cols].astype(jnp.bfloat16)
            gsend[2 * m + 1, :, :piece_cols] = term[:, piece_cols:].astype(jnp.bfloat16)
        each_peer(lambda k: send_term(k).start())
        gbuf[grp * SHARDS + me] = gsend[me]
        swap_term(me).start()

    def hand_on(first, last):
        def one(k):
            pltpu.make_async_copy(gbuf.at[grp * SHARDS + k], gbuf.at[grp * SHARDS + k], g_recv.at[k]).wait()
            swap_term(k).start()
        each_peer(one, -1, first, last)

    middle = SHARDS // 2

    def turn(j, _):
        with_planes(j, plane_step)
        with_planes(j - 1, row_step)
        pl.when(j < 2)(lambda: pick(1 + j * (middle - 1), middle + j * middle))
        with_planes(j - 1, group_step)
        pl.when(j == 2)(adapt)
        with_planes(j - 2, corner_step)
        with_planes(j - 2, core_step)
        pl.when((j == 3) | (j == 4))(
            lambda: hand_on(1 + (j - 3) * (middle - 1), middle + (j - 3) * middle))
        with_planes(j - 2, compute_step)
        return 0

    lax.fori_loop(0, PLANES + 2, turn, 0)
    keys_ref[...] = acc[...].astype(jnp.bfloat16)

    def drain(d, _):
        with_planes(d, drain_step)
        return 0

    lax.fori_loop(0, PLANES, drain, 0)
    each_peer(lambda k: send_piece(k).wait_send())
    each_peer(lambda k: send_term(k).wait_send())

    def swapped(k, _):
        other = gbuf.at[(1 - grp) * SHARDS + k]
        lend(k).wait_send()
        swap_term(k).wait_send()
        pltpu.make_async_copy(other, other, xg_recv.at[k]).wait()
        return 0

    lax.fori_loop(0, SHARDS, swapped, 0)


def sum_kernel(slots_ref, term_ref, out_ref):
    out_ref[...] = jnp.zeros_like(out_ref)
    slot_count = out_ref.shape[0]
    first = lax.axis_index("grp") * slot_count

    def one(t, _):
        slot = slots_ref[t] - first

        @pl.when((slot >= 0) & (slot < slot_count))
        def _():
            out_ref[slot] += term_ref[t, :, :out_ref.shape[2]].astype(jnp.float32)

        return 0

    lax.fori_loop(0, term_ref.shape[0], one, 0)


def on_block(tokens, cotangent, frozen_weight, adapters, tile_job, job_slot):
    table = jnp.arange(job_slot.shape[0], dtype=jnp.int32)
    slots = jnp.sum(jnp.where(tile_job == table[None, :], job_slot[None, :], 0), axis=1).astype(jnp.int32)
    adapters_t = jnp.swapaxes(adapters, 1, 2)
    slot_count, rank, piece_cols = adapters_t.shape
    tiles = slots.shape[0]
    wide = -(-piece_cols // 128) * 128
    rows, width = tokens.shape
    key_columns = cotangent.shape[1]
    shard_rows = frozen_weight.shape[0]
    halves = frozen_weight.reshape(2, shard_rows // 2, key_columns)
    vmem = pl.BlockSpec(memory_space=pltpu.VMEM)
    place = pl.BlockSpec(memory_space=pl.ANY)
    smem = pl.BlockSpec(memory_space=pltpu.SMEM)
    bf16 = jnp.bfloat16
    dma = pltpu.SemaphoreType.DMA
    keys, token_gradient, terms = pl.pallas_call(
        exchange_kernel,
        out_shape=(
            jax.ShapeDtypeStruct((rows, key_columns), bf16),
            jax.ShapeDtypeStruct((rows, width), bf16),
            jax.ShapeDtypeStruct((tiles, rank, wide), bf16),
        ),
        in_specs=[smem, place, place, place, place],
        out_specs=(vmem, vmem, vmem),
        scratch_shapes=[
            pltpu.VMEM(tokens.shape, bf16),
            pltpu.VMEM(cotangent.shape, bf16),
            pltpu.VMEM(adapters_t.shape, bf16),
            pltpu.VMEM((SHARDS, 2, shard_rows // 2, key_columns), bf16),
            pltpu.VMEM((SHARDS, rank, wide), bf16),
            pltpu.VMEM((SHARDS, rank, wide), bf16),
            pltpu.VMEM((SHARDS, rank, wide), bf16),
            pltpu.VMEM((SHARDS, rank, wide), bf16),
            pltpu.VMEM((rank, SHARDS * piece_cols), bf16),
            pltpu.VMEM((SHARDS, rank, wide), bf16),
            pltpu.VMEM((rows, key_columns), jnp.float32),
            pltpu.VMEM((rows, rank), bf16),
            pltpu.VMEM((key_columns, rows), bf16),
            dma((SHARDS * 5,)), dma((2 * SHARDS,)), dma((3,)), dma((SHARDS,)), dma((SHARDS,)),
            dma((SHARDS,)), dma((SHARDS,)), dma((SHARDS,)), dma((SHARDS,)), dma((SHARDS,)), dma((SHARDS,)),
        ],
        compiler_params=pltpu.CompilerParams(
            collective_id=0, has_side_effects=True, vmem_limit_bytes=60 * 1024 * 1024),
        name="exchange",
    )(slots, tokens, cotangent, halves, adapters_t)
    grads = pl.pallas_call(
        sum_kernel,
        out_shape=jax.ShapeDtypeStruct((slot_count, rank, piece_cols), jnp.float32),
        in_specs=[smem, vmem],
        out_specs=vmem,
        compiler_params=pltpu.CompilerParams(vmem_limit_bytes=24 * 1024 * 1024),
        name="slot_sums",
    )(slots, terms)
    return keys, token_gradient, jnp.swapaxes(grads, 1, 2)


def on_device(tokens, cotangent, frozen_weight, adapters, tile_job, job_slot):
    rank_width = tokens.shape[1]
    key_columns = cotangent.shape[1]
    rank = adapters.shape[2]
    slot_count = adapters.shape[0]
    row_count = adapters.shape[1]
    total_jobs = job_slot.shape[0]
    groups = lax.axis_size("grp")
    shards = lax.axis_size("seq")
    tiles_dev = tokens.shape[0] // TILE_ROWS
    group_index = lax.axis_index("grp")
    jobs = tile_job[:, 0]
    table = jnp.arange(total_jobs, dtype=jnp.int32)
    slots_all = jnp.sum(jnp.where(jobs[:, None] == table[None, :], job_slot[None, :], 0), axis=1)
    slots_all = slots_all.reshape(groups, shards, tiles_dev)
    group_slots = lax.dynamic_index_in_dim(slots_all, group_index, 0, keepdims=False)
    tile_slots = group_slots.T
    piece = lax.all_gather(frozen_weight, "seq", axis=0, tiled=True)
    forward_pass = jnp.dot(tokens, piece, preferred_element_type=jnp.float32)
    weight_update = jnp.einsum("nk,dk->nd", cotangent, piece, preferred_element_type=jnp.float32)
    owners = jnp.transpose(slots_all // slot_count, (0, 2, 1))
    local_slots = jnp.transpose(slots_all % slot_count, (0, 2, 1))
    picked = jnp.take(adapters, local_slots, axis=0)
    outgoing = jnp.where((owners == group_index)[..., None, None], picked, jnp.zeros_like(picked))
    arrived = lax.all_to_all(
        lax.all_to_all(outgoing, "grp", split_axis=0, concat_axis=0, tiled=True),
        "seq",
        split_axis=2,
        concat_axis=2,
        tiled=True,
    )
    fetched = jnp.sum(arrived.astype(jnp.float32), axis=0).astype(jnp.bfloat16)
    adapter_full = fetched.reshape(tiles_dev, shards * row_count, rank)
    down_weight = adapter_full[:, :rank_width]
    up_weight = adapter_full[:, rank_width:]
    token_tiles = tokens.reshape(tiles_dev, TILE_ROWS, rank_width)
    cot_tiles = cotangent.reshape(tiles_dev, TILE_ROWS, key_columns)
    hidden_width = jnp.einsum(
        "tnd,tdr->tnr", token_tiles, down_weight, preferred_element_type=jnp.float32
    ).astype(jnp.bfloat16)
    adapter_weights = jnp.einsum(
        "mhw,mow->mho", hidden_width, up_weight, preferred_element_type=jnp.float32
    )
    keys = (forward_pass + adapter_scale * adapter_weights.reshape(-1, key_columns)).astype(
        jnp.bfloat16
    )
    backward_pass = jnp.einsum(
        "tnk,tkr->tnr", cot_tiles, up_weight, preferred_element_type=jnp.float32
    ).astype(jnp.bfloat16)
    pass_through = jnp.einsum(
        "tnr,tdr->tnd", backward_pass, down_weight, preferred_element_type=jnp.float32
    )
    token_gradient = (weight_update + adapter_scale * pass_through.reshape(-1, rank_width)).astype(
        jnp.bfloat16
    )
    down_term = adapter_scale * jnp.einsum(
        "tnd,tnr->tdr", token_tiles, backward_pass, preferred_element_type=jnp.float32
    )
    up_term = adapter_scale * jnp.einsum(
        "tnk,tnr->tkr", cot_tiles, hidden_width, preferred_element_type=jnp.float32
    )
    terms = jnp.concatenate([down_term, up_term], axis=1).reshape(
        tiles_dev, shards, row_count, rank
    )
    incoming = lax.all_to_all(terms, "seq", split_axis=1, concat_axis=1, tiled=True)
    selector = (tile_slots.reshape(-1)[None, :] == table[:, None]).astype(jnp.float32)
    sums = jnp.dot(
        selector,
        incoming.reshape(tiles_dev * shards, row_count * rank),
        precision=lax.Precision.HIGHEST,
        preferred_element_type=jnp.float32,
    )
    owned = lax.psum_scatter(
        sums.reshape(total_jobs, row_count, rank), "grp", scatter_dimension=0, tiled=True
    )
    return (keys, token_gradient, owned)


def solution(mesh):
    placed = (
        P(("grp", "seq"), None),
        P(("grp", "seq"), None),
        P("seq", None),
        P("grp", "seq", None),
        P(),
        P(),
    )
    laid_out = mesh.shape["grp"] == 2 and mesh.shape["seq"] == SHARDS
    return jax.shard_map(
        on_block if laid_out else on_device,
        mesh=mesh,
        in_specs=placed,
        out_specs=(P(("grp", "seq"), None), P(("grp", "seq"), None), P("grp", "seq", None)),
        check_vma=False,
    )
```

```python
import functools

import jax
import jax.numpy as jnp
from jax import lax
from jax.experimental import pallas as pl
from jax.experimental.pallas import tpu as pltpu
from jax.sharding import PartitionSpec as P

TILE_ROWS = 128
MESH = pl.DeviceIdType.MESH

adapter_scale = 0.5

PLANES = 4
SHARDS = 16


def nt_dot(a, b):
    return lax.dot_general(a, b, (((1,), (1,)), ((), ())), preferred_element_type=jnp.float32)


def dot(a, b):
    return jnp.dot(a, b, preferred_element_type=jnp.float32)


def exchange_kernel(
    slots_ref, tok_hbm, cot_hbm, w_ref, adp_hbm,
    keys_ref, tg_ref, gbuf,
    tok_ref, cot_ref, adp_ref,
    wbuf, lent, borrowed, picked, pieces, down_t, gsend, acc, back, cot_t,
    w_send, w_recv, own_sem, xa_send, xa_recv, a_send, a_recv, g_send, g_recv, xg_send, xg_recv,
):
    grp = lax.axis_index("grp")
    me = lax.axis_index("seq")
    core = me % 2
    row = (me // 2) % 2
    plane = me // 4
    slot_count, rank, piece_cols = adp_ref.shape
    width = tok_ref.shape[1]
    shard_rows = width // SHARDS

    barrier = pltpu.get_barrier_semaphore()
    def greet(p, _):
        pl.semaphore_signal(barrier, inc=1, device_id=(grp, (me + p) % SHARDS), device_id_type=MESH)
        return 0
    own_copies = [
        pltpu.make_async_copy(w_ref.at[h], wbuf.at[me, h], w_recv.at[me * 2 + h]) for h in range(2)
    ]
    adp_copy = pltpu.make_async_copy(adp_hbm, adp_ref, own_sem.at[0])
    tok_copy = pltpu.make_async_copy(tok_hbm, tok_ref, own_sem.at[1])
    cot_copy = pltpu.make_async_copy(cot_hbm, cot_ref, own_sem.at[2])
    for copy in (adp_copy, *own_copies, tok_copy, cot_copy):
        copy.start()
    lax.fori_loop(1, SHARDS, greet, 0)
    pl.semaphore_signal(barrier, inc=1, device_id=(1 - grp, me), device_id_type=MESH)
    adp_copy.wait()

    def each_peer(do, away=1, first=1, last=SHARDS):
        def one(p, _):
            do((me + away * p) % SHARDS)
            return 0
        lax.fori_loop(first, last, one, 0)

    def lend(t):
        return pltpu.make_async_remote_copy(
            lent.at[t], borrowed.at[t], xa_send.at[t], xa_recv.at[t],
            device_id=(1 - grp, me), device_id_type=MESH)

    def local_of(tile):
        local = slots_ref[tile] - grp * slot_count
        held = jnp.minimum(jnp.maximum(local, 0), slot_count - 1)
        return local == held, held

    def pick_lent(t, _):
        lent[t, :, :piece_cols] = adp_ref[local_of((1 - grp) * SHARDS + t)[1]]
        return 0

    edge = piece_cols // 128 * 128
    for buf in (lent, picked, gsend):
        buf[:, :, edge:] = jnp.zeros_like(buf[:, :, edge:])
    lax.fori_loop(0, SHARDS, pick_lent, 0)
    pl.semaphore_wait(barrier, SHARDS)
    each_peer(lambda t: lend(t).start())
    lend(me).start()

    def send_w(p, y, h, kind):
        s = p * 4 + y * 2 + core
        target = (
            (grp, me + 4), (grp, me - 4),
            (grp, plane * 4 + (1 - row) * 2 + core),
            (1 - grp, me),
            (grp, plane * 4 + row * 2 + 1 - core),
        )[kind]
        return pltpu.make_async_remote_copy(
            wbuf.at[s, h], wbuf.at[s, h],
            w_send.at[((p * 2 + y) * 2 + h) * 5 + kind], w_recv.at[s * 2 + h],
            device_id=target, device_id_type=MESH)

    def take_w(s, h):
        pltpu.make_async_copy(wbuf.at[s, h], wbuf.at[s, h], w_recv.at[s * 2 + h]).wait()

    def with_planes(d, do):
        for sign in (-1, 1):
            p = plane + sign * d
            ok = (d >= 0) & (p >= 0) & (p < PLANES)
            if sign > 0:
                ok = ok & (d > 0)
            pl.when(ok)(functools.partial(do, p))

    def along_planes(p, h, act, reach=PLANES):
        @pl.when((p <= plane) & (plane < PLANES - 1) & (plane + 1 - p <= reach))
        def _():
            act(send_w(p, row, h, 0))

        @pl.when((p >= plane) & (plane > 0) & (p - plane + 1 <= reach))
        def _():
            act(send_w(p, row, h, 1))

    def start(copy):
        copy.start()

    def finish(copy):
        copy.wait_send()

    near = PLANES - 3

    def whole(p):
        return (p == plane) | ((core == 0) & (p - plane <= near) & (plane - p <= near))

    def from_plane(p, act):
        along_planes(p, grp, act)
        pl.when(core == 0)(lambda: along_planes(p, 1 - grp, act, near))
        act(send_w(p, row, grp, 2))
        pl.when(~whole(p))(lambda: act(send_w(p, row, grp, 3)))
        act(send_w(p, row, grp, 4))
        pl.when(whole(p))(lambda: act(send_w(p, row, 1 - grp, 4)))

    def from_group(p, act):
        @pl.when(~whole(p))
        def _():
            act(send_w(p, row, 1 - grp, 2))
            act(send_w(p, row, 1 - grp, 4))

        @pl.when(whole(p))
        def _():
            act(send_w(p, 1 - row, 1 - grp, 4))

    def from_row(p, act):
        pl.when(whole(p))(lambda: act(send_w(p, 1 - row, grp, 3)))
        act(send_w(p, 1 - row, grp, 4))

    def from_corner(p, act):
        pl.when(~whole(p))(lambda: act(send_w(p, 1 - row, 1 - grp, 4)))

    def plane_step(p):
        take_w(p * 4 + row * 2 + core, grp)
        pl.when(whole(p))(lambda: take_w(p * 4 + row * 2 + core, 1 - grp))
        from_plane(p, start)

    def group_step(p):
        pl.when(~whole(p))(lambda: take_w(p * 4 + row * 2 + core, 1 - grp))
        pl.when(whole(p))(lambda: take_w(p * 4 + (1 - row) * 2 + core, 1 - grp))
        from_group(p, start)

    def row_step(p):
        take_w(p * 4 + (1 - row) * 2 + core, grp)
        from_row(p, start)

    def corner_step(p):
        pl.when(~whole(p))(lambda: take_w(p * 4 + (1 - row) * 2 + core, 1 - grp))
        from_corner(p, start)

    def core_step(p):
        for y in range(2):
            for h in range(2):
                take_w(p * 4 + y * 2 + 1 - core, h)

    def drain_step(p):
        for leaves in (from_plane, from_group, from_row, from_corner):
            leaves(p, finish)

    def compute_step(p):
        def shard(i, _):
            s = p * 4 + i
            cols = pl.ds(pl.multiple_of(s * shard_rows, shard_rows), shard_rows)
            block = wbuf[s].reshape(shard_rows, cot_ref.shape[1])
            acc[...] += dot(tok_ref[:, cols], block)
            grad = dot(block, cot_t[...]).T + adapter_scale * dot(back[...], down_t[:, cols])
            tg_ref[:, cols] = grad.astype(jnp.bfloat16)
            return 0

        lax.fori_loop(0, 4, shard, 0)

    def send_piece(k):
        return pltpu.make_async_remote_copy(
            picked.at[k], pieces.at[me], a_send.at[k], a_recv.at[me],
            device_id=(grp, k), device_id_type=MESH)

    def send_term(k):
        return pltpu.make_async_remote_copy(
            gsend.at[k], gbuf.at[grp * SHARDS + me], g_send.at[k], g_recv.at[me],
            device_id=(grp, k), device_id_type=MESH)

    def swap_term(k):
        return pltpu.make_async_remote_copy(
            gbuf.at[grp * SHARDS + k], gbuf.at[grp * SHARDS + k], xg_send.at[k], xg_recv.at[k],
            device_id=(1 - grp, me), device_id_type=MESH)

    def pick(first, last):
        def choose(t):
            lend(t).wait_recv()
            owned, held = local_of(grp * SHARDS + t)
            picked[t, :, :piece_cols] = jnp.where(
                owned, adp_ref[held], borrowed[t, :, :piece_cols])

        def one(t):
            choose(t)
            send_piece(t).start()

        each_peer(one, 1, first, last)

        @pl.when(last == SHARDS)
        def _():
            choose(me)
            pieces[me] = picked[me]

    def adapt():
        tok_copy.wait()
        cot_copy.wait()
        each_peer(lambda k: pltpu.make_async_copy(pieces.at[k], pieces.at[k], a_recv.at[k]).wait(), -1)
        pair = 2 * piece_cols
        for m in range(SHARDS // 2):
            down_t[:, m * pair:(m + 1) * pair] = jnp.concatenate(
                [pieces[2 * m, :, :piece_cols], pieces[2 * m + 1, :, :piece_cols]], axis=1)
        up = down_t[:, width:]
        hidden = jnp.zeros((TILE_ROWS, rank), jnp.float32)
        step = width // 4
        for q in range(4):
            t_cols = tok_ref[:, q * step:(q + 1) * step]
            d_cols = down_t[:, q * step:(q + 1) * step]
            hidden = hidden + nt_dot(t_cols, d_cols)
        hidden_t = hidden.T.astype(jnp.bfloat16)
        hidden = hidden.astype(jnp.bfloat16)
        back_wide = nt_dot(cot_ref[...], up)
        back[...] = back_wide.astype(jnp.bfloat16)
        back_t = back_wide.T.astype(jnp.bfloat16)
        cot_t[...] = cot_ref[...].T
        acc[...] = adapter_scale * dot(hidden, up)
        for m in range(SHARDS // 2):
            first, last = m * pair, (m + 1) * pair
            if last <= width:
                term = dot(back_t, tok_ref[:, first:last])
            else:
                term = jnp.concatenate(
                    [dot(back_t, tok_ref[:, first:width]), dot(hidden_t, cot_ref[:, :last - width])], axis=1)
            term = adapter_scale * term
            gsend[2 * m, :, :piece_cols] = term[:, :piece_cols].astype(jnp.bfloat16)
            gsend[2 * m + 1, :, :piece_cols] = term[:, piece_cols:].astype(jnp.bfloat16)
        each_peer(lambda k: send_term(k).start())
        gbuf[grp * SHARDS + me] = gsend[me]
        swap_term(me).start()

    def hand_on(first, last):
        def one(k):
            pltpu.make_async_copy(gbuf.at[grp * SHARDS + k], gbuf.at[grp * SHARDS + k], g_recv.at[k]).wait()
            swap_term(k).start()
        each_peer(one, -1, first, last)

    middle = SHARDS // 2

    def turn(j, _):
        with_planes(j, plane_step)
        with_planes(j - 1, row_step)
        pl.when(j < 2)(lambda: pick(1 + j * (middle - 1), middle + j * middle))
        with_planes(j - 1, group_step)
        pl.when(j == 2)(adapt)
        with_planes(j - 2, corner_step)
        with_planes(j - 2, core_step)
        pl.when((j == 3) | (j == 4))(
            lambda: hand_on(1 + (j - 3) * (middle - 1), middle + (j - 3) * middle))
        with_planes(j - 2, compute_step)
        return 0

    lax.fori_loop(0, PLANES + 2, turn, 0)
    keys_ref[...] = acc[...].astype(jnp.bfloat16)

    def drain(d, _):
        with_planes(d, drain_step)
        return 0

    lax.fori_loop(0, PLANES, drain, 0)
    each_peer(lambda k: send_piece(k).wait_send())
    each_peer(lambda k: send_term(k).wait_send())

    def swapped(k, _):
        other = gbuf.at[(1 - grp) * SHARDS + k]
        lend(k).wait_send()
        swap_term(k).wait_send()
        pltpu.make_async_copy(other, other, xg_recv.at[k]).wait()
        return 0

    lax.fori_loop(0, SHARDS, swapped, 0)


def sum_kernel(slots_ref, term_ref, out_ref):
    out_ref[...] = jnp.zeros_like(out_ref)
    slot_count = out_ref.shape[0]
    first = lax.axis_index("grp") * slot_count

    def one(t, _):
        slot = slots_ref[t] - first

        @pl.when((slot >= 0) & (slot < slot_count))
        def _():
            out_ref[slot] += term_ref[t, :, :out_ref.shape[2]].astype(jnp.float32)

        return 0

    lax.fori_loop(0, term_ref.shape[0], one, 0)


def on_block(tokens, cotangent, frozen_weight, adapters, tile_job, job_slot):
    table = jnp.arange(job_slot.shape[0], dtype=jnp.int32)
    slots = jnp.sum(jnp.where(tile_job == table[None, :], job_slot[None, :], 0), axis=1).astype(jnp.int32)
    adapters_t = jnp.swapaxes(adapters, 1, 2)
    slot_count, rank, piece_cols = adapters_t.shape
    tiles = slots.shape[0]
    wide = -(-piece_cols // 128) * 128
    rows, width = tokens.shape
    key_columns = cotangent.shape[1]
    shard_rows = frozen_weight.shape[0]
    halves = frozen_weight.reshape(2, shard_rows // 2, key_columns)
    vmem = pl.BlockSpec(memory_space=pltpu.VMEM)
    place = pl.BlockSpec(memory_space=pl.ANY)
    smem = pl.BlockSpec(memory_space=pltpu.SMEM)
    bf16 = jnp.bfloat16
    dma = pltpu.SemaphoreType.DMA
    keys, token_gradient, terms = pl.pallas_call(
        exchange_kernel,
        out_shape=(
            jax.ShapeDtypeStruct((rows, key_columns), bf16),
            jax.ShapeDtypeStruct((rows, width), bf16),
            jax.ShapeDtypeStruct((tiles, rank, wide), bf16),
        ),
        in_specs=[smem, place, place, place, place],
        out_specs=(vmem, vmem, vmem),
        scratch_shapes=[
            pltpu.VMEM(tokens.shape, bf16),
            pltpu.VMEM(cotangent.shape, bf16),
            pltpu.VMEM(adapters_t.shape, bf16),
            pltpu.VMEM((SHARDS, 2, shard_rows // 2, key_columns), bf16),
            pltpu.VMEM((SHARDS, rank, wide), bf16),
            pltpu.VMEM((SHARDS, rank, wide), bf16),
            pltpu.VMEM((SHARDS, rank, wide), bf16),
            pltpu.VMEM((SHARDS, rank, wide), bf16),
            pltpu.VMEM((rank, SHARDS * piece_cols), bf16),
            pltpu.VMEM((SHARDS, rank, wide), bf16),
            pltpu.VMEM((rows, key_columns), jnp.float32),
            pltpu.VMEM((rows, rank), bf16),
            pltpu.VMEM((key_columns, rows), bf16),
            dma((SHARDS * 5,)), dma((2 * SHARDS,)), dma((3,)), dma((SHARDS,)), dma((SHARDS,)),
            dma((SHARDS,)), dma((SHARDS,)), dma((SHARDS,)), dma((SHARDS,)), dma((SHARDS,)), dma((SHARDS,)),
        ],
        compiler_params=pltpu.CompilerParams(
            collective_id=0, has_side_effects=True, vmem_limit_bytes=60 * 1024 * 1024),
        name="exchange",
    )(slots, tokens, cotangent, halves, adapters_t)
    grads = pl.pallas_call(
        sum_kernel,
        out_shape=jax.ShapeDtypeStruct((slot_count, rank, piece_cols), jnp.float32),
        in_specs=[smem, vmem],
        out_specs=vmem,
        compiler_params=pltpu.CompilerParams(vmem_limit_bytes=24 * 1024 * 1024),
        name="slot_sums",
    )(slots, terms)
    return keys, token_gradient, jnp.swapaxes(grads, 1, 2)


def on_device(tokens, cotangent, frozen_weight, adapters, tile_job, job_slot):
    rank_width = tokens.shape[1]
    key_columns = cotangent.shape[1]
    rank = adapters.shape[2]
    slot_count = adapters.shape[0]
    row_count = adapters.shape[1]
    total_jobs = job_slot.shape[0]
    groups = lax.axis_size("grp")
    shards = lax.axis_size("seq")
    tiles_dev = tokens.shape[0] // TILE_ROWS
    group_index = lax.axis_index("grp")
    jobs = tile_job[:, 0]
    table = jnp.arange(total_jobs, dtype=jnp.int32)
    slots_all = jnp.sum(jnp.where(jobs[:, None] == table[None, :], job_slot[None, :], 0), axis=1)
    slots_all = slots_all.reshape(groups, shards, tiles_dev)
    group_slots = lax.dynamic_index_in_dim(slots_all, group_index, 0, keepdims=False)
    tile_slots = group_slots.T
    piece = lax.all_gather(frozen_weight, "seq", axis=0, tiled=True)
    forward_pass = jnp.dot(tokens, piece, preferred_element_type=jnp.float32)
    weight_update = jnp.einsum("nk,dk->nd", cotangent, piece, preferred_element_type=jnp.float32)
    owners = jnp.transpose(slots_all // slot_count, (0, 2, 1))
    local_slots = jnp.transpose(slots_all % slot_count, (0, 2, 1))
    picked = jnp.take(adapters, local_slots, axis=0)
    outgoing = jnp.where((owners == group_index)[..., None, None], picked, jnp.zeros_like(picked))
    arrived = lax.all_to_all(
        lax.all_to_all(outgoing, "grp", split_axis=0, concat_axis=0, tiled=True),
        "seq",
        split_axis=2,
        concat_axis=2,
        tiled=True,
    )
    fetched = jnp.sum(arrived.astype(jnp.float32), axis=0).astype(jnp.bfloat16)
    adapter_full = fetched.reshape(tiles_dev, shards * row_count, rank)
    down_weight = adapter_full[:, :rank_width]
    up_weight = adapter_full[:, rank_width:]
    token_tiles = tokens.reshape(tiles_dev, TILE_ROWS, rank_width)
    cot_tiles = cotangent.reshape(tiles_dev, TILE_ROWS, key_columns)
    hidden_width = jnp.einsum(
        "tnd,tdr->tnr", token_tiles, down_weight, preferred_element_type=jnp.float32
    ).astype(jnp.bfloat16)
    adapter_weights = jnp.einsum(
        "mhw,mow->mho", hidden_width, up_weight, preferred_element_type=jnp.float32
    )
    keys = (forward_pass + adapter_scale * adapter_weights.reshape(-1, key_columns)).astype(
        jnp.bfloat16
    )
    backward_pass = jnp.einsum(
        "tnk,tkr->tnr", cot_tiles, up_weight, preferred_element_type=jnp.float32
    ).astype(jnp.bfloat16)
    pass_through = jnp.einsum(
        "tnr,tdr->tnd", backward_pass, down_weight, preferred_element_type=jnp.float32
    )
    token_gradient = (weight_update + adapter_scale * pass_through.reshape(-1, rank_width)).astype(
        jnp.bfloat16
    )
    down_term = adapter_scale * jnp.einsum(
        "tnd,tnr->tdr", token_tiles, backward_pass, preferred_element_type=jnp.float32
    )
    up_term = adapter_scale * jnp.einsum(
        "tnk,tnr->tkr", cot_tiles, hidden_width, preferred_element_type=jnp.float32
    )
    terms = jnp.concatenate([down_term, up_term], axis=1).reshape(
        tiles_dev, shards, row_count, rank
    )
    incoming = lax.all_to_all(terms, "seq", split_axis=1, concat_axis=1, tiled=True)
    selector = (tile_slots.reshape(-1)[None, :] == table[:, None]).astype(jnp.float32)
    sums = jnp.dot(
        selector,
        incoming.reshape(tiles_dev * shards, row_count * rank),
        precision=lax.Precision.HIGHEST,
        preferred_element_type=jnp.float32,
    )
    owned = lax.psum_scatter(
        sums.reshape(total_jobs, row_count, rank), "grp", scatter_dimension=0, tiled=True
    )
    return (keys, token_gradient, owned)


def solution(mesh):
    placed = (
        P(("grp", "seq"), None),
        P(("grp", "seq"), None),
        P("seq", None),
        P("grp", "seq", None),
        P(),
        P(),
    )
    laid_out = mesh.shape["grp"] == 2 and mesh.shape["seq"] == SHARDS
    return jax.shard_map(
        on_block if laid_out else on_device,
        mesh=mesh,
        in_specs=placed,
        out_specs=(P(("grp", "seq"), None), P(("grp", "seq"), None), P("grp", "seq", None)),
        check_vma=False,
    )
```
